32 devices in a mesh: phi: 4 (over x, core), eta: 8 (over z, y).
Axes of the slice: x: 2, y: 2, z: 4, core: 2. Of those that a mesh axis runs over, the one named last changes fastest.
Arguments:
- query: bfloat16 [192, 16384], P(None, ('phi', 'eta')), may hold values from -64 to 64
- key_rows: bfloat16 [192, 16384], P(None, ('phi', 'eta')), may hold values from -6 to 6
- value: bfloat16 [192, 16384], P(None, ('phi', 'eta')), may hold values from -6 to 6
- out_grad: bfloat16 [192, 16384], P(None, ('phi', 'eta')), may hold values from -6 to 6
- members: int32 [3, 128, 128], P(None, ('phi', 'eta')), may hold values from 0 to 16383, as said below
Outputs:
- query_grad: bfloat16 [192, 16384], P(None, ('phi', 'eta'))
- key_grad: bfloat16 [192, 16384], P(None, ('phi', 'eta'))
- value_grad: bfloat16 [192, 16384], P(None, ('phi', 'eta'))
The draws below stay inside these ranges and needn't reach their ends.
Inputs may be any that keep to these rules, and one draw needn't show every extreme that they name: `members`: bucket i of every table is owned by device i // 4 in the order phi+eta, and point id j lies on device j // 512. In each table every point id appears exactly once. In one table a device's buckets hold at most 20 points of any one source device, and exactly 20 for some pairs of devices.
All inputs are finite; a program needn't handle non-finite values.
Results may differ from the reference program's by a relative error of at most 0.0097.
Values may be sent and summed in bfloat16 or wider, within the bound.
No kernel may reach another device: no remote copies, remote signals or barrier semaphores. Data moves between devices by JAX's collectives and lax.ppermute only.
A program may use at most 64 MiB of HBM per device.

```python
import jax
import jax.numpy as jnp
from jax import lax

HEADS = 8
HEAD_DIM = 24
FEAT = 192
TABLES = 3
BUCKET = 128
P_DEV = 512
OWNERS = 32
POINTS = 16384
BUCK_DEV = 4
NBUCK = 128
CAP = 20


def member_table(key):
    key_one, key_two, key_three = jax.random.split(key, 3)
    offsets = jax.random.permutation(key_one, OWNERS).astype(jnp.int32)
    device_no = jnp.arange(OWNERS, dtype=jnp.int32)
    quarter = OWNERS // 4
    base_count = P_DEV // OWNERS
    weights = jnp.where(device_no < quarter, CAP, jnp.where(device_no < 2 * quarter, base_count - base_count // 4, base_count)).astype(jnp.int32)
    ending = jnp.cumsum(weights).astype(jnp.int32)
    position = jnp.arange(P_DEV, dtype=jnp.int32)
    section_of = jnp.sum((ending[None, :] <= position[:, None]).astype(jnp.int32), axis=1)
    source = (device_no[:, None] - offsets[section_of][None, :]) % OWNERS
    shuffle = jax.vmap(lambda subkey: jax.random.permutation(subkey, P_DEV))(jax.random.split(key_two, OWNERS)).astype(jnp.int32)
    local_ids = shuffle[source, position[None, :]]
    point_ids = source * P_DEV + local_ids
    placing = jax.vmap(lambda subkey: jax.random.permutation(subkey, P_DEV))(jax.random.split(key_three, OWNERS)).astype(jnp.int32)
    point_ids = jnp.take_along_axis(point_ids, placing, axis=1)
    return point_ids.reshape(NBUCK, BUCKET).astype(jnp.int32)


def draw_members(key, part):
    return jnp.stack([member_table(jax.random.fold_in(key, table_no)) for table_no in range(TABLES)])


def draw_query(key, part):
    key_one = jax.random.fold_in(key, 0)
    sample = jnp.clip(jax.random.normal(key_one, (FEAT, POINTS), jnp.float32), -6.0, 6.0)
    return sample.astype(jnp.bfloat16)


def levels(key, shape, shards, low, high):
    def one(dim, blocks):
        draws = jax.random.uniform(jax.random.fold_in(jax.random.fold_in(key, 6), dim), (blocks,), jnp.float32, low / len(shards), high / len(shards))
        return jnp.repeat(jnp.exp(draws), shape[dim] // blocks).reshape((-1,) + (1,) * (len(shape) - dim - 1))

    loudness = one(*shards[0])
    for cut in shards[1:]:
        loudness = loudness * one(*cut)
    return loudness


def noise(key, extent, deviation, bound, cuts=(), kind=jnp.bfloat16):
    entries = deviation * jax.random.normal(key, extent, jnp.float32)
    if cuts:
        entries = entries * levels(key, extent, cuts, -0.22, 0.18)
    return jnp.clip(entries, -bound, bound).astype(kind)


def setup_inputs(seed: int = 0) -> dict:
    arg_keys = jax.random.split(jax.random.key(seed), 6)
    return {
        "query": draw_query(jax.random.fold_in(arg_keys[5], 71), 0),
        "key_rows": noise(arg_keys[1], (FEAT, POINTS), 1.0, 6.0, ((1, 32),)),
        "value": noise(arg_keys[2], (FEAT, POINTS), 1.0, 6.0, ((1, 32),)),
        "out_grad": noise(arg_keys[3], (FEAT, POINTS), 1.0, 6.0, ((1, 32),)),
        "members": draw_members(jax.random.fold_in(arg_keys[5], 71), 0),
    }


def bucket_grads(query_part, key_part, value_part, grad_part):
    scale = HEAD_DIM ** -0.5
    query_full = query_part.astype(jnp.float32)
    key_full = key_part.astype(jnp.float32)
    value_full = value_part.astype(jnp.float32)
    grad_full = grad_part.astype(jnp.float32)
    dots = jnp.einsum('bihd,bjhd->bhij', query_full, key_full)
    key_norm = jnp.einsum('bjhd,bjhd->bhj', key_full, key_full)
    scores = scale * (dots - 0.5 * key_norm[:, :, None, :])
    row_max = jnp.max(scores, axis=-1, keepdims=True)
    expons = jnp.exp(scores - row_max)
    probs = expons / jnp.sum(expons, axis=-1, keepdims=True)
    probs_low = probs.astype(jnp.bfloat16).astype(jnp.float32)
    outputs = jnp.einsum('bhij,bjhd->bihd', probs_low, value_full)
    delta = jnp.sum(grad_full * outputs, axis=-1)
    dprob = jnp.einsum('bihd,bjhd->bhij', grad_full, value_full)
    dscore = scale * probs * (dprob - jnp.transpose(delta, (0, 2, 1))[..., None])
    dscore_low = dscore.astype(jnp.bfloat16).astype(jnp.float32)
    query_grad = jnp.einsum('bhij,bjhd->bihd', dscore_low, key_full)
    column_sums = jnp.transpose(jnp.sum(dscore, axis=2), (0, 2, 1))[..., None]
    key_grad = jnp.einsum('bhij,bihd->bjhd', dscore_low, query_full) - column_sums * key_full
    value_grad = jnp.einsum('bhij,bihd->bjhd', probs_low, grad_full)
    shape_rows = (query_part.shape[0], query_part.shape[1], HEADS * HEAD_DIM)
    return jnp.concatenate([query_grad.reshape(shape_rows).astype(jnp.bfloat16),
                            key_grad.reshape(shape_rows).astype(jnp.bfloat16),
                            value_grad.reshape(shape_rows).astype(jnp.bfloat16)], axis=-1)


def reference(query, key_rows, value, out_grad, members):
    width = HEADS * HEAD_DIM
    query_rows = query.T
    key_points = key_rows.T
    value_rows = value.T
    grad_rows = out_grad.T
    summed = jnp.zeros((POINTS, 3 * width), jnp.float32)
    for table_no in range(TABLES):
        group_ids = members[table_no].reshape(OWNERS, BUCK_DEV, BUCKET).astype(jnp.int32)

        def one_group(bucket_ids):
            shape_heads = (BUCK_DEV, BUCKET, HEADS, HEAD_DIM)
            return bucket_grads(query_rows[bucket_ids].reshape(shape_heads), key_points[bucket_ids].reshape(shape_heads),
                                value_rows[bucket_ids].reshape(shape_heads), grad_rows[bucket_ids].reshape(shape_heads))

        gradient = lax.map(one_group, group_ids)
        summed = summed.at[group_ids.reshape(-1)].add(gradient.reshape(-1, 3 * width).astype(jnp.float32))
    result = summed.astype(jnp.bfloat16).T
    return (result[:width], result[width:2 * width], result[2 * width:])
```

```python
import functools

import jax
import jax.numpy as jnp
from jax import lax
from jax.experimental import pallas as pl
from jax.experimental.pallas import tpu as pltpu
from jax.sharding import PartitionSpec as P

HEADS = 8
AXES = ("phi", "eta")
LOG2E = 1.4426950408889634
VMEM_BYTES = 48 * 1024 * 1024


def dot(a, b, da, db):
    return lax.dot_general(a, b, (((da,), (db,)), ((), ())), preferred_element_type=jnp.float32)


def column_of(row):
    n = row.shape[1]
    diagonal = lax.broadcasted_iota(jnp.int32, (n, n), 0) == lax.broadcasted_iota(jnp.int32, (n, n), 1)
    return jnp.sum(jnp.where(diagonal, jnp.broadcast_to(row, (n, n)), 0.0), axis=1, keepdims=True)


def one_hot_rows(column, width):
    n = column.shape[0]
    places = lax.broadcasted_iota(jnp.int32, (n, width), 1).astype(jnp.float32)
    return jnp.where(column == places, 1.0, 0.0).astype(jnp.bfloat16)


def slots_of(lids_ref, points):
    group = lids_ref.shape[0]
    lids = lids_ref[...].astype(jnp.float32)
    return jnp.concatenate([one_hot_rows(column_of(lids[o : o + 1]), points) for o in range(group)], axis=0)


def pack_kernel(lids_ref, q_ref, k_ref, v_ref, g_ref, out_ref):
    group, rows, width = out_ref.shape
    features = jnp.concatenate([q_ref[...], k_ref[...], v_ref[...], g_ref[...]], axis=0)
    picks = slots_of(lids_ref, features.shape[1])
    packed = dot(picks, features, 1, 1)
    out_ref[...] = packed.astype(jnp.bfloat16).reshape(group, rows, width)


def fold_kernel(lids_ref, replies_ref, out_ref):
    group, rows, width = replies_ref.shape
    picks = slots_of(lids_ref, out_ref.shape[1])
    out_ref[...] = dot(replies_ref[...].reshape(group * rows, width), picks, 0, 0).astype(jnp.bfloat16)


def finish_kernel(lids_ref, replies_ref, other_ref, q_ref, k_ref, v_ref):
    group, rows, width = replies_ref.shape
    picks = slots_of(lids_ref, other_ref.shape[1])
    total = dot(replies_ref[...].reshape(group * rows, width), picks, 0, 0) + other_ref[...].astype(jnp.float32)
    total = total.astype(jnp.bfloat16)
    third = width // 3
    q_ref[...] = total[:third]
    k_ref[...] = total[third : 2 * third]
    v_ref[...] = total[2 * third :]


def attend_kernel(windows, codes_ref, own_ref, other_ref, out_own_ref, out_other_ref, feats_ref, grads_ref):
    group, rows, width4 = own_ref.shape
    feat = width4 // 4
    head_dim = feat // HEADS
    scale = head_dim**-0.5
    tables, points = codes_ref.shape
    buckets = points // 128
    pair = 2 * head_dim
    head_of = lax.broadcasted_iota(jnp.int32, (pair, 256), 0) // head_dim
    block_of = lax.broadcasted_iota(jnp.int32, (pair, 256), 1) // 128
    mask = jnp.where(head_of == block_of, 1.0, 0.0).astype(jnp.bfloat16)

    def blocked(part):
        return jnp.concatenate([part, part], axis=1) * mask

    out_own_ref[...] = jnp.zeros_like(out_own_ref)
    out_other_ref[...] = jnp.zeros_like(out_other_ref)
    for t in range(tables):
        low, high = windows[t]
        span = high - low
        slots = 2 * group * span
        codes = codes_ref[t : t + 1, :].astype(jnp.float32)
        columns = jnp.concatenate([column_of(codes[:, b * 128 : (b + 1) * 128]) for b in range(buckets)], axis=0)
        picks = one_hot_rows(columns, slots)
        arrived = jnp.concatenate(
            [ref[:, low:high, :].reshape(group * span, width4) for ref in (own_ref, other_ref)], axis=0
        )
        feats_ref[...] = dot(picks, arrived, 1, 0).T.astype(jnp.bfloat16)

        def bucket(b, carry):
            lanes = pl.ds(pl.multiple_of(b * 128, 128), 128)
            for h in range(HEADS // 2):
                at = h * pair
                q = feats_ref[at : at + pair, lanes]
                k = feats_ref[feat + at : feat + at + pair, lanes]
                v = feats_ref[2 * feat + at : 2 * feat + at + pair, lanes]
                g = feats_ref[3 * feat + at : 3 * feat + at + pair, lanes]
                k_wide = k.astype(jnp.float32)
                k_block = blocked(k)
                squares = k_wide * k_wide
                norms = [
                    (0.5 * scale * LOG2E) * jnp.sum(squares[i * head_dim : (i + 1) * head_dim], axis=0, keepdims=True)
                    for i in range(2)
                ]
                scores = dot(q, k_block, 0, 0)
                dprob = dot(g, blocked(v), 0, 0)
                probs_low, dscore_low, sums = [], [], []
                for i in range(2):
                    cols = slice(i * 128, (i + 1) * 128)
                    logits = scores[:, cols] * (scale * LOG2E) - norms[i]
                    logits = logits - jnp.max(logits, axis=1, keepdims=True)
                    expons = jnp.exp2(logits)
                    probs = expons * (1.0 / jnp.sum(expons, axis=1, keepdims=True))
                    delta = jnp.sum(probs * dprob[:, cols], axis=1, keepdims=True)
                    dscore = probs * (dprob[:, cols] - delta)
                    probs_low.append(probs.astype(jnp.bfloat16))
                    dscore_low.append(dscore.astype(jnp.bfloat16))
                    sums.append(jnp.broadcast_to(jnp.sum(dscore, axis=0, keepdims=True), (head_dim, 128)))
                dscore_wide = jnp.concatenate(dscore_low, axis=1)
                dscore_tall = jnp.concatenate(dscore_low, axis=0)
                probs_tall = jnp.concatenate(probs_low, axis=0)
                dq = scale * dot(k_block, dscore_wide, 1, 1)
                dk = scale * (dot(blocked(q), dscore_tall, 1, 0) - jnp.concatenate(sums, axis=0) * k_wide)
                dv = dot(blocked(g), probs_tall, 1, 0)
                grads_ref[at : at + pair, lanes] = dq.astype(jnp.bfloat16)
                grads_ref[feat + at : feat + at + pair, lanes] = dk.astype(jnp.bfloat16)
                grads_ref[2 * feat + at : 2 * feat + at + pair, lanes] = dv.astype(jnp.bfloat16)
            return carry

        lax.fori_loop(0, buckets, bucket, 0)
        grads = grads_ref[...]
        for part, ref in enumerate((out_own_ref, out_other_ref)):
            places = lax.broadcasted_iota(jnp.int32, (group * span, points), 0).astype(jnp.float32) + float(
                part * group * span
            )
            back = jnp.where(places == codes, 1.0, 0.0).astype(jnp.bfloat16)
            rows_back = dot(back, grads, 1, 1).astype(jnp.bfloat16).reshape(group, span, 3 * feat)
            ref[:, low:high, :] = ref[:, low:high, :] + rows_back


def call(kernel, out_shape, scratch=(), flops=0, moved=0):
    return pl.pallas_call(
        kernel,
        out_shape=out_shape,
        scratch_shapes=list(scratch),
        compiler_params=pltpu.CompilerParams(vmem_limit_bytes=VMEM_BYTES),
        cost_estimate=pl.CostEstimate(flops=flops, bytes_accessed=moved, transcendentals=0),
    )


def on_device(query, key_rows, value, out_grad, members):
    points = query.shape[1]
    feat = query.shape[0]
    tables = members.shape[0]
    phi, eta = lax.axis_size("phi"), lax.axis_size("eta")
    owners = phi * eta
    half = eta // 2
    group = phi * half
    capacity = 5 * points // (4 * owners)
    rows = -(-tables * capacity // 16) * 16
    windows = [
        (t * capacity // 16 * 16, -(-(t * capacity + capacity) // 16) * 16) for t in range(tables)
    ]
    halves = [[p * eta + h * half + e for p in range(phi) for e in range(half)] for h in range(2)]
    across = [(p * eta + e, p * eta + (e + half) % eta) for p in range(phi) for e in range(eta)]

    def exchange(chunks):
        return lax.all_to_all(chunks, AXES, 0, 0, tiled=True, axis_index_groups=halves)

    bf16 = jnp.bfloat16
    arrays = (query, key_rows, value, out_grad)
    copies = [lax.ppermute(array, AXES, across) for array in arrays]

    ids = members.reshape(tables, points)
    home, local = ids // points, ids % points
    position = jnp.arange(points, dtype=jnp.int32)
    same = home[:, :, None] == home[:, None, :]
    earlier = position[None, :, None] > position[None, None, :]
    rank = jnp.sum((same & earlier).astype(jnp.int32), axis=2)
    home_p, home_e = home // eta, home % eta
    part = (home_e // half != lax.axis_index("eta") // half).astype(jnp.int32)
    place = home_p * half + home_e % half
    table = jnp.arange(tables, dtype=jnp.int32)[:, None]
    slot = (place * 2 + part) * rows + table * capacity + rank
    slots = jnp.arange(group * 2 * rows, dtype=jnp.int32)
    match = slots[:, None] == slot.reshape(1, -1)
    wanted = jnp.sum(jnp.where(match, local.reshape(1, -1) + 1, 0), axis=1) - 1
    lids = exchange(wanted.reshape(group, 2, rows))
    lows = jnp.array([low for low, _ in windows], jnp.int32)[:, None]
    spans = jnp.array([high - low for low, high in windows], jnp.int32)[:, None]
    codes = (part * group + place) * spans + table * capacity + rank - lows

    packed = jax.ShapeDtypeStruct((group, rows, 4 * feat), bf16)
    reply = jax.ShapeDtypeStruct((group, rows, 3 * feat), bf16)
    column = jax.ShapeDtypeStruct((feat, points), bf16)
    pack = call(pack_kernel, packed, flops=2 * group * rows * points * 4 * feat, moved=2 * group * rows * 4 * feat)
    arrived_own = exchange(pack(lids[:, 0], *arrays))
    arrived_other = exchange(pack(lids[:, 1], *copies))
    attend = call(
        functools.partial(attend_kernel, windows),
        (reply, reply),
        scratch=(pltpu.VMEM((4 * feat, points), bf16), pltpu.VMEM((3 * feat, points), bf16)),
        flops=2 * 10**10,
        moved=8 * 10**6,
    )
    reply_own, reply_other = attend(codes, arrived_own, arrived_other)
    returned_other = exchange(reply_other)
    fold = call(
        fold_kernel,
        jax.ShapeDtypeStruct((3 * feat, points), bf16),
        flops=2 * group * rows * points * 3 * feat,
        moved=2 * group * rows * 3 * feat,
    )
    summed = lax.ppermute(fold(lids[:, 1], returned_other), AXES, across)
    returned_own = exchange(reply_own)
    finish = call(
        finish_kernel,
        (column, column, column),
        flops=2 * group * rows * points * 3 * feat,
        moved=2 * group * rows * 3 * feat,
    )
    return finish(lids[:, 0], returned_own, summed)


def solution(mesh):
    split = P(None, AXES)
    in_specs = (split, split, split, split, P(None, AXES, None))
    return jax.shard_map(
        on_device, mesh=mesh, in_specs=in_specs, out_specs=(split, split, split), check_vma=False
    )
```

```python
import functools

import jax
import jax.numpy as jnp
from jax import lax
from jax.experimental import pallas as pl
from jax.experimental.pallas import tpu as pltpu
from jax.sharding import PartitionSpec as P

HEADS = 8
BUCKET = 128
AXES = ("phi", "eta")
LOG2E = 1.4426950408889634
VMEM_BYTES = 48 * 1024 * 1024
PACK_FLOPS = 4 * 10**10


def dot(a, b, da, db):
    return lax.dot_general(a, b, (((da,), (db,)), ((), ())), preferred_element_type=jnp.float32)


def column_of(row, first, count):
    n = row.shape[1]
    diagonal = lax.broadcasted_iota(jnp.int32, (count, n), 0) + first == lax.broadcasted_iota(jnp.int32, (count, n), 1)
    return jnp.sum(jnp.where(diagonal, jnp.broadcast_to(row, (count, n)), 0.0), axis=1, keepdims=True)


def slots_of(wanted_ref, part, rows, points):
    group = wanted_ref.shape[0]
    wanted = wanted_ref[...].astype(jnp.float32)
    places = lax.broadcasted_iota(jnp.int32, (rows, points), 1).astype(jnp.float32)
    picks = [
        jnp.where(column_of(wanted[o, :1], part * rows, rows) == places, 1.0, 0.0).astype(jnp.bfloat16)
        for o in range(group)
    ]
    return jnp.concatenate(picks, axis=0)


def index_kernel(sizes, half_ref, members_ref, wanted_ref, codes_ref):
    windows, capacity, rows, eta = sizes
    tables, buckets, _ = members_ref.shape
    points = buckets * BUCKET
    group = wanted_ref.shape[0]
    half = eta // 2
    f32, bf16 = jnp.float32, jnp.bfloat16
    ids = jnp.concatenate([members_ref[:, b, :] for b in range(buckets)], axis=1).astype(f32)
    home = jnp.floor((ids + 0.5) * (1.0 / points))
    local = ids - home * points
    home_p = jnp.floor((home + 0.5) * (1.0 / eta))
    home_e = home - home_p * eta
    home_h = jnp.floor((home_e + 0.5) * (1.0 / half))
    part = jnp.where(home_h == half_ref[0, 0].astype(f32), 0.0, 1.0)
    place = home_p * half + home_e - home_h * half
    before = lax.broadcasted_iota(jnp.int32, (points, points), 0) < lax.broadcasted_iota(jnp.int32, (points, points), 1)
    before = jnp.where(before, 1.0, 0.0).astype(bf16)
    homes = lax.broadcasted_iota(jnp.int32, (2 * group, points), 0).astype(f32)
    holders = lax.broadcasted_iota(jnp.int32, (group, points), 0).astype(f32)
    lanes = lax.broadcasted_iota(jnp.int32, (2 * rows, points), 0).astype(f32)
    total = jnp.zeros((2 * group, 2 * rows), f32)
    for t in range(tables):
        row = slice(t, t + 1)
        hot = jnp.where(homes == home[row], 1.0, 0.0)
        rank = jnp.sum(hot * dot(hot.astype(bf16), before, 1, 0), axis=0, keepdims=True)
        slot = rank + float(t * capacity)
        low, high = windows[t]
        code = (part[row] * float(group) + place[row]) * float(high - low) + slot - float(low)
        codes_ref[row, :] = code.astype(jnp.int32)
        named = local[row] + 1.0
        large = jnp.floor(named * (1.0 / 256.0)) * 256.0
        held = holders == place[row]
        values = jnp.concatenate([jnp.where(held, large, 0.0), jnp.where(held, named - large, 0.0)], axis=0)
        at = jnp.where(lanes == part[row] * float(rows) + slot, 1.0, 0.0)
        total += dot(values.astype(bf16), at.astype(bf16), 1, 1)
    wanted = (total[:group] + total[group:] - 1.0).astype(jnp.int32)
    for o in range(group):
        wanted_ref[o] = jnp.broadcast_to(wanted[o : o + 1], wanted_ref.shape[1:])


def pack_kernel(part, wanted_ref, q_ref, k_ref, v_ref, g_ref, out_ref, features_ref, sems):
    group, rows, width = out_ref.shape
    feat, points = q_ref.shape
    copies = [
        pltpu.make_async_copy(ref, features_ref.at[pl.ds(n * feat, feat)], sems.at[n])
        for n, ref in enumerate((q_ref, k_ref, v_ref, g_ref))
    ]
    for copy in copies:
        copy.start()
    picks = slots_of(wanted_ref, part, rows, points)
    for copy in copies:
        copy.wait()
    packed = dot(picks, features_ref[...], 1, 1)
    out_ref[...] = packed.astype(jnp.bfloat16).reshape(group, rows, width)


def fold_kernel(wanted_ref, replies_ref, out_ref):
    group, rows, width = replies_ref.shape
    picks = slots_of(wanted_ref, 1, rows, out_ref.shape[1])
    out_ref[...] = dot(replies_ref[...].reshape(group * rows, width), picks, 0, 0).astype(jnp.bfloat16)


def finish_kernel(wanted_ref, replies_ref, other_ref, q_ref, k_ref, v_ref):
    group, rows, width = replies_ref.shape
    picks = slots_of(wanted_ref, 0, rows, other_ref.shape[1])
    total = dot(replies_ref[...].reshape(group * rows, width), picks, 0, 0) + other_ref[...].astype(jnp.float32)
    total = total.astype(jnp.bfloat16)
    third = width // 3
    q_ref[...] = total[:third]
    k_ref[...] = total[third : 2 * third]
    v_ref[...] = total[2 * third :]


def attend_kernel(
    windows,
    codes_ref,
    own_ref,
    other_ref,
    out_own_ref,
    out_other_ref,
    feats_ref,
    grads_ref,
    scores_ref,
    dprobs_ref,
    probs_ref,
    dscores_ref,
    falls_ref,
):
    group, rows, width4 = own_ref.shape
    feat = width4 // 4
    head_dim = feat // HEADS
    scale = head_dim**-0.5
    tables, points = codes_ref.shape
    buckets = points // BUCKET
    pair = 2 * head_dim
    bf16 = jnp.bfloat16
    head_of = lax.broadcasted_iota(jnp.int32, (pair, 2 * BUCKET), 0) // head_dim
    block_of = lax.broadcasted_iota(jnp.int32, (pair, 2 * BUCKET), 1) // BUCKET
    mask = jnp.where(head_of == block_of, 1.0, 0.0).astype(bf16)
    tail = lax.broadcasted_iota(jnp.int32, (16, BUCKET), 0)
    tail_wide = lax.broadcasted_iota(jnp.int32, (16, 2 * BUCKET), 0)
    tail_block = lax.broadcasted_iota(jnp.int32, (16, 2 * BUCKET), 1) // BUCKET
    halves = jnp.where((tail_wide < 6) & (tail_wide // 3 == tail_block), -0.5, 0.0).astype(bf16)
    lane = lax.broadcasted_iota(jnp.int32, (BUCKET, BUCKET), 1)

    def blocked(part):
        return jnp.concatenate([part, part], axis=1) * mask

    def norm_rows(k):
        wide = k.astype(jnp.float32)
        squares = wide * wide
        first, second = (
            jnp.sum(squares[i * head_dim : (i + 1) * head_dim], axis=0, keepdims=True) for i in range(2)
        )
        norm = jnp.where(tail < 3, first, second)
        high = norm.astype(bf16).astype(jnp.float32)
        rest = norm - high
        middle = rest.astype(bf16).astype(jnp.float32)
        piece = tail % 3
        out = jnp.where(piece == 0, high, jnp.where(piece == 1, middle, rest - middle))
        return jnp.where(tail < 6, out, 0.0).astype(bf16)

    out_own_ref[...] = jnp.zeros_like(out_own_ref)
    out_other_ref[...] = jnp.zeros_like(out_other_ref)
    todo = [(b, h) for b in range(buckets) for h in range(HEADS // 2)]
    for t in range(tables):
        low, high = windows[t]
        span = high - low
        slots = 2 * group * span
        codes = codes_ref[t : t + 1, :].astype(jnp.float32)
        places = lax.broadcasted_iota(jnp.int32, (slots, points), 0).astype(jnp.float32)
        picks = jnp.where(places == codes, 1.0, 0.0).astype(bf16)
        arrived = jnp.concatenate(
            [ref[:, low:high, :].reshape(group * span, width4) for ref in (own_ref, other_ref)], axis=0
        )
        feats_ref[...] = dot(arrived, picks, 0, 0).astype(bf16)

        def part_of(which, b, h):
            at = which * feat + h * pair
            return feats_ref[at : at + pair, b * BUCKET : (b + 1) * BUCKET]

        for n, (b, h) in enumerate(todo):
            q, k, v, g = (part_of(which, b, h) for which in range(4))
            scores_ref[n] = dot(
                jnp.concatenate([k, norm_rows(k)], axis=0), jnp.concatenate([blocked(q), halves], axis=0), 0, 0
            )
            dprobs_ref[n] = dot(v, blocked(g), 0, 0)
        for n in range(len(todo)):
            for i in range(2):
                cols = slice(i * BUCKET, (i + 1) * BUCKET)
                dprob = dprobs_ref[n, :, cols]
                scores = scores_ref[n, :, cols]
                expons = jnp.exp2((scores - jnp.max(scores, axis=0, keepdims=True)) * (scale * LOG2E))
                probs = expons * (1.0 / jnp.sum(expons, axis=0, keepdims=True))
                delta = jnp.sum(probs * dprob, axis=0, keepdims=True)
                dscore = probs * (dprob - delta)
                probs_ref[n, :, cols] = probs.astype(bf16)
                dscores_ref[n, :, cols] = dscore.astype(bf16)
                falls_ref[n, i] = jnp.broadcast_to(jnp.sum(dscore, axis=1, keepdims=True), (BUCKET, BUCKET))
        for n, (b, h) in enumerate(todo):
            if h == 0:
                falls = sum(
                    jnp.where(lane == i, falls_ref[b * (HEADS // 2) + i // 2, i % 2], 0.0) for i in range(HEADS)
                ).T
            q, k, g = (part_of(which, b, h) for which in (0, 1, 3))
            dscore_tall = jnp.concatenate([dscores_ref[n, :, :BUCKET], dscores_ref[n, :, BUCKET:]], axis=0)
            dq = scale * dot(blocked(k), dscore_tall, 1, 0)
            fall = jnp.concatenate(
                [jnp.broadcast_to(falls[i : i + 1], (head_dim, BUCKET)) for i in (2 * h, 2 * h + 1)], axis=0
            )
            dk = scale * (dot(blocked(q), dscores_ref[n], 1, 1) - fall * k.astype(jnp.float32))
            dv = dot(blocked(g), probs_ref[n], 1, 1)
            for which, grad in enumerate((dq, dk, dv)):
                at = which * feat + h * pair
                grads_ref[at : at + pair, b * BUCKET : (b + 1) * BUCKET] = grad.astype(bf16)
        back = dot(picks, grads_ref[...], 1, 1).astype(bf16).reshape(2, group, span, 3 * feat)
        for part, ref in enumerate((out_own_ref, out_other_ref)):
            ref[:, low:high, :] = ref[:, low:high, :] + back[part]


def call(kernel, out_shape, scratch=(), flops=0, moved=0, in_specs=None):
    extra = {} if in_specs is None else {"in_specs": in_specs}
    return pl.pallas_call(
        kernel,
        out_shape=out_shape,
        scratch_shapes=list(scratch),
        compiler_params=pltpu.CompilerParams(vmem_limit_bytes=VMEM_BYTES),
        cost_estimate=pl.CostEstimate(flops=flops, bytes_accessed=moved, transcendentals=0),
        **extra,
    )


def on_device(query, key_rows, value, out_grad, members):
    feat, points = query.shape
    tables = members.shape[0]
    phi, eta = lax.axis_size("phi"), lax.axis_size("eta")
    half = eta // 2
    group = phi * half
    capacity = 5 * points // (4 * phi * eta)
    rows = -(-tables * capacity // 16) * 16
    windows = [(t * capacity // 16 * 16, -(-(t * capacity + capacity) // 16) * 16) for t in range(tables)]
    halves = [[p * eta + h * half + e for p in range(phi) for e in range(half)] for h in range(2)]
    across = [(p * eta + e, p * eta + (e + half) % eta) for p in range(phi) for e in range(eta)]
    bf16 = jnp.bfloat16
    packed = jax.ShapeDtypeStruct((group, rows, 4 * feat), bf16)
    reply = jax.ShapeDtypeStruct((group, rows, 3 * feat), bf16)
    column = jax.ShapeDtypeStruct((feat, points), bf16)
    steps = points // BUCKET * (HEADS // 2)
    vmem = pl.BlockSpec(memory_space=pltpu.VMEM)

    def exchange(chunks):
        return lax.all_to_all(chunks, AXES, 0, 0, tiled=True, axis_index_groups=halves)

    def pack(part, flops):
        return call(
            functools.partial(pack_kernel, part),
            packed,
            scratch=(pltpu.VMEM((4 * feat, points), bf16), pltpu.SemaphoreType.DMA((4,))),
            in_specs=[vmem] + [pl.BlockSpec(memory_space=pltpu.HBM)] * 4,
            flops=flops,
            moved=2 * group * rows * 4 * feat,
        )

    arrays = (query, key_rows, value, out_grad)
    copies = [lax.ppermute(array, AXES, across) for array in arrays]

    index = call(
        functools.partial(index_kernel, (windows, capacity, rows, eta)),
        (
            jax.ShapeDtypeStruct((group, 8, 2 * rows), jnp.int32),
            jax.ShapeDtypeStruct((tables, points), jnp.int32),
        ),
        in_specs=[pl.BlockSpec(memory_space=pltpu.SMEM), vmem],
        flops=10**9,
        moved=10**5,
    )
    wanted, codes = index((lax.axis_index("eta") // half).astype(jnp.int32).reshape(1, 1), members)
    wanted = exchange(wanted)

    arrived_own = exchange(pack(0, 2 * group * rows * points * 4 * feat)(wanted, *arrays))
    arrived_other = exchange(pack(1, PACK_FLOPS)(wanted, *copies))
    attend = call(
        functools.partial(attend_kernel, windows),
        (reply, reply),
        scratch=(
            pltpu.VMEM((4 * feat, points), bf16),
            pltpu.VMEM((3 * feat, points), bf16),
            pltpu.VMEM((steps, BUCKET, 2 * BUCKET), jnp.float32),
            pltpu.VMEM((steps, BUCKET, 2 * BUCKET), jnp.float32),
            pltpu.VMEM((steps, BUCKET, 2 * BUCKET), bf16),
            pltpu.VMEM((steps, BUCKET, 2 * BUCKET), bf16),
            pltpu.VMEM((steps, 2, BUCKET, BUCKET), jnp.float32),
        ),
        flops=2 * 10**10,
        moved=8 * 10**6,
    )
    reply_own, reply_other = attend(codes, arrived_own, arrived_other)
    returned_other = exchange(reply_other)
    fold = call(
        fold_kernel,
        jax.ShapeDtypeStruct((3 * feat, points), bf16),
        flops=2 * group * rows * points * 3 * feat,
        moved=2 * group * rows * 3 * feat,
    )
    folded, reply_own = lax.optimization_barrier((fold(wanted, returned_other), reply_own))
    summed = lax.ppermute(folded, AXES, across)
    returned_own = exchange(reply_own)
    finish = call(
        finish_kernel,
        (column, column, column),
        flops=2 * group * rows * points * 3 * feat,
        moved=2 * group * rows * 3 * feat,
    )
    return finish(wanted, returned_own, summed)


def solution(mesh):
    split = P(None, AXES)
    in_specs = (split, split, split, split, P(None, AXES, None))
    return jax.shard_map(
        on_device, mesh=mesh, in_specs=in_specs, out_specs=(split, split, split), check_vma=False
    )
```

```python
import functools

import jax
import jax.numpy as jnp
from jax import lax
from jax.experimental import pallas as pl
from jax.experimental.pallas import tpu as pltpu
from jax.sharding import PartitionSpec as P

HEADS = 8
BUCKET = 128
AXES = ("phi", "eta")
LOG2E = 1.4426950408889634
VMEM_BYTES = 48 * 1024 * 1024
PACK_FLOPS = 4 * 10**10


def dot(a, b, da, db):
    return lax.dot_general(a, b, (((da,), (db,)), ((), ())), preferred_element_type=jnp.float32)


def column_of(row, first, count):
    n = row.shape[1]
    diagonal = lax.broadcasted_iota(jnp.int32, (count, n), 0) + first == lax.broadcasted_iota(jnp.int32, (count, n), 1)
    return jnp.sum(jnp.where(diagonal, jnp.broadcast_to(row, (count, n)), 0.0), axis=1, keepdims=True)


def slots_of(wanted_ref, part, rows, points):
    group = wanted_ref.shape[0]
    wanted = wanted_ref[...].astype(jnp.float32)
    places = lax.broadcasted_iota(jnp.int32, (rows, points), 1).astype(jnp.float32)
    picks = [
        jnp.where(column_of(wanted[o, :1], part * rows, rows) == places, 1.0, 0.0).astype(jnp.bfloat16)
        for o in range(group)
    ]
    return jnp.concatenate(picks, axis=0)


def index_kernel(sizes, half_ref, members_ref, wanted_ref, codes_ref):
    windows, capacity, rows, eta = sizes
    tables, buckets, _ = members_ref.shape
    points = buckets * BUCKET
    group = wanted_ref.shape[0]
    half = eta // 2
    f32, bf16 = jnp.float32, jnp.bfloat16
    ids = jnp.concatenate([members_ref[:, b, :] for b in range(buckets)], axis=1).astype(f32)
    home = jnp.floor((ids + 0.5) * (1.0 / points))
    local = ids - home * points
    home_p = jnp.floor((home + 0.5) * (1.0 / eta))
    home_e = home - home_p * eta
    home_h = jnp.floor((home_e + 0.5) * (1.0 / half))
    part = jnp.where(home_h == half_ref[0, 0].astype(f32), 0.0, 1.0)
    within = home_e - home_h * half
    deep = jnp.floor((within + 0.5) * (2.0 / half))
    place = home_p * half + within + part * (0.5 * half) * (1.0 - 2.0 * deep)
    before = lax.broadcasted_iota(jnp.int32, (points, points), 0) < lax.broadcasted_iota(jnp.int32, (points, points), 1)
    before = jnp.where(before, 1.0, 0.0).astype(bf16)
    homes = lax.broadcasted_iota(jnp.int32, (2 * group, points), 0).astype(f32)
    holders = lax.broadcasted_iota(jnp.int32, (group, points), 0).astype(f32)
    lanes = lax.broadcasted_iota(jnp.int32, (2 * rows, points), 0).astype(f32)
    total = jnp.zeros((2 * group, 2 * rows), f32)
    for t in range(tables):
        row = slice(t, t + 1)
        hot = jnp.where(homes == home[row], 1.0, 0.0)
        rank = jnp.sum(hot * dot(hot.astype(bf16), before, 1, 0), axis=0, keepdims=True)
        slot = rank + float(t * capacity)
        low, high = windows[t]
        code = (part[row] * float(group) + place[row]) * float(high - low) + slot - float(low)
        codes_ref[row, :] = code.astype(jnp.int32)
        named = local[row] + 1.0
        large = jnp.floor(named * (1.0 / 256.0)) * 256.0
        held = holders == place[row]
        values = jnp.concatenate([jnp.where(held, large, 0.0), jnp.where(held, named - large, 0.0)], axis=0)
        at = jnp.where(lanes == part[row] * float(rows) + slot, 1.0, 0.0)
        total += dot(values.astype(bf16), at.astype(bf16), 1, 1)
    wanted = (total[:group] + total[group:] - 1.0).astype(jnp.int32)
    for o in range(group):
        wanted_ref[o] = jnp.broadcast_to(wanted[o : o + 1], wanted_ref.shape[1:])


def pack_kernel(part, wanted_ref, q_ref, k_ref, v_ref, g_ref, out_ref, features_ref, sems):
    group, rows, width = out_ref.shape
    feat, points = q_ref.shape
    copies = [
        pltpu.make_async_copy(ref, features_ref.at[pl.ds(n * feat, feat)], sems.at[n])
        for n, ref in enumerate((q_ref, k_ref, v_ref, g_ref))
    ]
    for copy in copies:
        copy.start()
    picks = slots_of(wanted_ref, part, rows, points)
    for copy in copies:
        copy.wait()
    packed = dot(picks, features_ref[...], 1, 1)
    out_ref[...] = packed.astype(jnp.bfloat16).reshape(group, rows, width)


def fold_kernel(wanted_ref, replies_ref, out_ref):
    group, rows, width = replies_ref.shape
    picks = slots_of(wanted_ref, 1, rows, out_ref.shape[1])
    out_ref[...] = dot(replies_ref[...].reshape(group * rows, width), picks, 0, 0).astype(jnp.bfloat16)


def finish_kernel(wanted_ref, replies_ref, other_ref, q_ref, k_ref, v_ref):
    group, rows, width = replies_ref.shape
    picks = slots_of(wanted_ref, 0, rows, other_ref.shape[1])
    total = dot(replies_ref[...].reshape(group * rows, width), picks, 0, 0) + other_ref[...].astype(jnp.float32)
    total = total.astype(jnp.bfloat16)
    third = width // 3
    q_ref[...] = total[:third]
    k_ref[...] = total[third : 2 * third]
    v_ref[...] = total[2 * third :]


def attend_kernel(
    windows,
    codes_ref,
    own_ref,
    other_ref,
    out_own_ref,
    out_other_ref,
    feats_ref,
    grads_ref,
    scores_ref,
    dprobs_ref,
    probs_ref,
    dscores_ref,
    falls_ref,
):
    group, rows, width4 = own_ref.shape
    feat = width4 // 4
    head_dim = feat // HEADS
    scale = head_dim**-0.5
    tables, points = codes_ref.shape
    buckets = points // BUCKET
    pair = 2 * head_dim
    bf16 = jnp.bfloat16
    head_of = lax.broadcasted_iota(jnp.int32, (pair, 2 * BUCKET), 0) // head_dim
    block_of = lax.broadcasted_iota(jnp.int32, (pair, 2 * BUCKET), 1) // BUCKET
    mask = jnp.where(head_of == block_of, 1.0, 0.0).astype(bf16)
    tail = lax.broadcasted_iota(jnp.int32, (16, BUCKET), 0)
    tail_wide = lax.broadcasted_iota(jnp.int32, (16, 2 * BUCKET), 0)
    tail_block = lax.broadcasted_iota(jnp.int32, (16, 2 * BUCKET), 1) // BUCKET
    halves = jnp.where((tail_wide < 6) & (tail_wide // 3 == tail_block), -0.5, 0.0).astype(bf16)
    lane = lax.broadcasted_iota(jnp.int32, (BUCKET, BUCKET), 1)

    def blocked(part):
        return jnp.concatenate([part, part], axis=1) * mask

    def norm_rows(k):
        wide = k.astype(jnp.float32)
        squares = wide * wide
        first, second = (
            jnp.sum(squares[i * head_dim : (i + 1) * head_dim], axis=0, keepdims=True) for i in range(2)
        )
        norm = jnp.where(tail < 3, first, second)
        high = norm.astype(bf16).astype(jnp.float32)
        rest = norm - high
        middle = rest.astype(bf16).astype(jnp.float32)
        piece = tail % 3
        out = jnp.where(piece == 0, high, jnp.where(piece == 1, middle, rest - middle))
        return jnp.where(tail < 6, out, 0.0).astype(bf16)

    out_own_ref[...] = jnp.zeros_like(out_own_ref)
    out_other_ref[...] = jnp.zeros_like(out_other_ref)
    todo = [(b, h) for b in range(buckets) for h in range(HEADS // 2)]
    for t in range(tables):
        low, high = windows[t]
        span = high - low
        slots = 2 * group * span
        codes = codes_ref[t : t + 1, :].astype(jnp.float32)
        places = lax.broadcasted_iota(jnp.int32, (slots, points), 0).astype(jnp.float32)
        picks = jnp.where(places == codes, 1.0, 0.0).astype(bf16)
        arrived = jnp.concatenate(
            [ref[:, low:high, :].reshape(group * span, width4) for ref in (own_ref, other_ref)], axis=0
        )
        feats_ref[...] = dot(arrived, picks, 0, 0).astype(bf16)

        def part_of(which, b, h):
            at = which * feat + h * pair
            return feats_ref[at : at + pair, b * BUCKET : (b + 1) * BUCKET]

        for n, (b, h) in enumerate(todo):
            q, k, v, g = (part_of(which, b, h) for which in range(4))
            scores_ref[n] = dot(
                jnp.concatenate([k, norm_rows(k)], axis=0), jnp.concatenate([blocked(q), halves], axis=0), 0, 0
            )
            dprobs_ref[n] = dot(v, blocked(g), 0, 0)
        for n in range(len(todo)):
            for i in range(2):
                cols = slice(i * BUCKET, (i + 1) * BUCKET)
                dprob = dprobs_ref[n, :, cols]
                scores = scores_ref[n, :, cols]
                expons = jnp.exp2((scores - jnp.max(scores, axis=0, keepdims=True)) * (scale * LOG2E))
                probs = expons * (1.0 / jnp.sum(expons, axis=0, keepdims=True))
                delta = jnp.sum(probs * dprob, axis=0, keepdims=True)
                dscore = probs * (dprob - delta)
                probs_ref[n, :, cols] = probs.astype(bf16)
                dscores_ref[n, :, cols] = dscore.astype(bf16)
                falls_ref[n, i] = jnp.broadcast_to(jnp.sum(dscore, axis=1, keepdims=True), (BUCKET, BUCKET))
        for n, (b, h) in enumerate(todo):
            if h == 0:
                falls = sum(
                    jnp.where(lane == i, falls_ref[b * (HEADS // 2) + i // 2, i % 2], 0.0) for i in range(HEADS)
                ).T
            q, k, g = (part_of(which, b, h) for which in (0, 1, 3))
            dscore_tall = jnp.concatenate([dscores_ref[n, :, :BUCKET], dscores_ref[n, :, BUCKET:]], axis=0)
            dq = scale * dot(blocked(k), dscore_tall, 1, 0)
            fall = jnp.concatenate(
                [jnp.broadcast_to(falls[i : i + 1], (head_dim, BUCKET)) for i in (2 * h, 2 * h + 1)], axis=0
            )
            dk = scale * (dot(blocked(q), dscores_ref[n], 1, 1) - fall * k.astype(jnp.float32))
            dv = dot(blocked(g), probs_ref[n], 1, 1)
            for which, grad in enumerate((dq, dk, dv)):
                at = which * feat + h * pair
                grads_ref[at : at + pair, b * BUCKET : (b + 1) * BUCKET] = grad.astype(bf16)
        back = dot(picks, grads_ref[...], 1, 1).astype(bf16).reshape(2, group, span, 3 * feat)
        for part, ref in enumerate((out_own_ref, out_other_ref)):
            ref[:, low:high, :] = ref[:, low:high, :] + back[part]


def call(kernel, out_shape, scratch=(), flops=0, moved=0, in_specs=None):
    extra = {} if in_specs is None else {"in_specs": in_specs}
    return pl.pallas_call(
        kernel,
        out_shape=out_shape,
        scratch_shapes=list(scratch),
        compiler_params=pltpu.CompilerParams(vmem_limit_bytes=VMEM_BYTES),
        cost_estimate=pl.CostEstimate(flops=flops, bytes_accessed=moved, transcendentals=0),
        **extra,
    )


def on_device(query, key_rows, value, out_grad, members):
    feat, points = query.shape
    tables = members.shape[0]
    phi, eta = lax.axis_size("phi"), lax.axis_size("eta")
    half = eta // 2
    group = phi * half
    capacity = 5 * points // (4 * phi * eta)
    rows = -(-tables * capacity // 16) * 16
    windows = [(t * capacity // 16 * 16, -(-(t * capacity + capacity) // 16) * 16) for t in range(tables)]
    halves = [[p * eta + h * half + e for p in range(phi) for e in range(half)] for h in range(2)]
    layer = eta // 4
    across = [
        (p * eta + z * layer + e, p * eta + (3 - z) * layer + e) for p in range(phi) for z in range(4) for e in range(layer)
    ]
    bf16 = jnp.bfloat16
    packed = jax.ShapeDtypeStruct((group, rows, 4 * feat), bf16)
    reply = jax.ShapeDtypeStruct((group, rows, 3 * feat), bf16)
    column = jax.ShapeDtypeStruct((feat, points), bf16)
    steps = points // BUCKET * (HEADS // 2)
    vmem = pl.BlockSpec(memory_space=pltpu.VMEM)

    def exchange(chunks):
        return lax.all_to_all(chunks, AXES, 0, 0, tiled=True, axis_index_groups=halves)

    def pack(part, flops):
        return call(
            functools.partial(pack_kernel, part),
            packed,
            scratch=(pltpu.VMEM((4 * feat, points), bf16), pltpu.SemaphoreType.DMA((4,))),
            in_specs=[vmem] + [pl.BlockSpec(memory_space=pltpu.HBM)] * 4,
            flops=flops,
            moved=2 * group * rows * 4 * feat,
        )

    arrays = (query, key_rows, value, out_grad)
    copies = [lax.ppermute(array, AXES, across) for array in arrays]

    index = call(
        functools.partial(index_kernel, (windows, capacity, rows, eta)),
        (
            jax.ShapeDtypeStruct((group, 8, 2 * rows), jnp.int32),
            jax.ShapeDtypeStruct((tables, points), jnp.int32),
        ),
        in_specs=[pl.BlockSpec(memory_space=pltpu.SMEM), vmem],
        flops=10**9,
        moved=10**5,
    )
    wanted, codes = index((lax.axis_index("eta") // half).astype(jnp.int32).reshape(1, 1), members)
    wanted = exchange(wanted)

    arrived_own = exchange(pack(0, 2 * group * rows * points * 4 * feat)(wanted, *arrays))
    arrived_other = exchange(pack(1, PACK_FLOPS)(wanted, *copies))
    attend = call(
        functools.partial(attend_kernel, windows),
        (reply, reply),
        scratch=(
            pltpu.VMEM((4 * feat, points), bf16),
            pltpu.VMEM((3 * feat, points), bf16),
            pltpu.VMEM((steps, BUCKET, 2 * BUCKET), jnp.float32),
            pltpu.VMEM((steps, BUCKET, 2 * BUCKET), jnp.float32),
            pltpu.VMEM((steps, BUCKET, 2 * BUCKET), bf16),
            pltpu.VMEM((steps, BUCKET, 2 * BUCKET), bf16),
            pltpu.VMEM((steps, 2, BUCKET, BUCKET), jnp.float32),
        ),
        flops=2 * 10**10,
        moved=8 * 10**6,
    )
    reply_own, reply_other = attend(codes, arrived_own, arrived_other)
    returned_other = exchange(reply_other)
    fold = call(
        fold_kernel,
        jax.ShapeDtypeStruct((3 * feat, points), bf16),
        flops=2 * group * rows * points * 3 * feat,
        moved=2 * group * rows * 3 * feat,
    )
    folded, reply_own = lax.optimization_barrier((fold(wanted, returned_other), reply_own))
    summed = lax.ppermute(folded, AXES, across)
    returned_own = exchange(reply_own)
    finish = call(
        finish_kernel,
        (column, column, column),
        flops=2 * group * rows * points * 3 * feat,
        moved=2 * group * rows * 3 * feat,
    )
    return finish(wanted, returned_own, summed)


def solution(mesh):
    split = P(None, AXES)
    in_specs = (split, split, split, split, P(None, AXES, None))
    return jax.shard_map(
        on_device, mesh=mesh, in_specs=in_specs, out_specs=(split, split, split), check_vma=False
    )
```

```python
import functools

import jax
import jax.numpy as jnp
from jax import lax
from jax.experimental import pallas as pl
from jax.experimental.pallas import tpu as pltpu
from jax.sharding import PartitionSpec as P

HEADS = 8
BUCKET = 128
AXES = ("phi", "eta")
LOG2E = 1.4426950408889634
VMEM_BYTES = 48 * 1024 * 1024
WHOLE_VMEM_BYTES = 60 * 1024 * 1024
PACK_FLOPS = 4 * 10**10
PACK_STEPS = 4


def dot(a, b, da, db):
    return lax.dot_general(a, b, (((da,), (db,)), ((), ())), preferred_element_type=jnp.float32)


def column_of(row, first, count):
    n = row.shape[1]
    diagonal = lax.broadcasted_iota(jnp.int32, (count, n), 0) + first == lax.broadcasted_iota(jnp.int32, (count, n), 1)
    return jnp.sum(jnp.where(diagonal, jnp.broadcast_to(row, (count, n)), 0.0), axis=1, keepdims=True)


def slots_of(wanted_ref, part, rows, points, owners=None):
    places = lax.broadcasted_iota(jnp.int32, (rows, points), 1).astype(jnp.float32)
    picks = []
    for o in range(wanted_ref.shape[0]) if owners is None else owners:
        wanted = wanted_ref[o, :1].astype(jnp.float32)
        picks.append(jnp.where(column_of(wanted, part * rows, rows) == places, 1.0, 0.0).astype(jnp.bfloat16))
    return jnp.concatenate(picks, axis=0)


def index_kernel(sizes, half_ref, members_ref, wanted_ref, codes_ref):
    windows, capacity, rows, eta = sizes
    tables, buckets, _ = members_ref.shape
    points = buckets * BUCKET
    group = wanted_ref.shape[0]
    half = eta // 2
    f32, bf16 = jnp.float32, jnp.bfloat16
    ids = jnp.concatenate([members_ref[:, b, :] for b in range(buckets)], axis=1).astype(f32)
    home = jnp.floor((ids + 0.5) * (1.0 / points))
    local = ids - home * points
    home_p = jnp.floor((home + 0.5) * (1.0 / eta))
    home_e = home - home_p * eta
    home_h = jnp.floor((home_e + 0.5) * (1.0 / half))
    part = jnp.where(home_h == half_ref[0, 0].astype(f32), 0.0, 1.0)
    within = home_e - home_h * half
    deep = jnp.floor((within + 0.5) * (2.0 / half))
    place = home_p * half + within + part * (0.5 * half) * (1.0 - 2.0 * deep)
    before = lax.broadcasted_iota(jnp.int32, (points, points), 0) < lax.broadcasted_iota(jnp.int32, (points, points), 1)
    before = jnp.where(before, 1.0, 0.0).astype(bf16)
    homes = lax.broadcasted_iota(jnp.int32, (2 * group, points), 0).astype(f32)
    holders = lax.broadcasted_iota(jnp.int32, (group, points), 0).astype(f32)
    lanes = lax.broadcasted_iota(jnp.int32, (2 * rows, points), 0).astype(f32)
    total = jnp.zeros((2 * group, 2 * rows), f32)
    for t in range(tables):
        row = slice(t, t + 1)
        hot = jnp.where(homes == home[row], 1.0, 0.0)
        rank = jnp.sum(hot * dot(hot.astype(bf16), before, 1, 0), axis=0, keepdims=True)
        slot = rank + float(t * capacity)
        low, high = windows[t]
        code = (part[row] * float(group) + place[row]) * float(high - low) + slot - float(low)
        codes_ref[row, :] = code.astype(jnp.int32)
        named = local[row] + 1.0
        large = jnp.floor(named * (1.0 / 256.0)) * 256.0
        held = holders == place[row]
        values = jnp.concatenate([jnp.where(held, large, 0.0), jnp.where(held, named - large, 0.0)], axis=0)
        at = jnp.where(lanes == part[row] * float(rows) + slot, 1.0, 0.0)
        total += dot(values.astype(bf16), at.astype(bf16), 1, 1)
    wanted = (total[:group] + total[group:] - 1.0).astype(jnp.int32)
    for o in range(group):
        wanted_ref[o] = jnp.broadcast_to(wanted[o : o + 1], wanted_ref.shape[1:])


def pack_kernel(part, wanted_ref, q_ref, k_ref, v_ref, g_ref, out_ref, features_ref, packed_ref, sems, out_sems):
    group, rows, width = out_ref.shape
    feat, points = q_ref.shape
    copies = [
        pltpu.make_async_copy(ref, features_ref.at[pl.ds(n * feat, feat)], sems.at[n])
        for n, ref in enumerate((q_ref, k_ref, v_ref, g_ref))
    ]
    for copy in copies:
        copy.start()
    share = group // PACK_STEPS
    picks = [
        slots_of(wanted_ref, part, rows, points, range(c * share, (c + 1) * share)) for c in range(PACK_STEPS)
    ]
    for copy in copies:
        copy.wait()
    features = features_ref[...]
    results = []
    for c in range(PACK_STEPS):
        packed = dot(picks[c], features, 1, 1).astype(jnp.bfloat16)
        packed_ref[c] = packed.reshape(share, rows, width)
        results.append(
            pltpu.make_async_copy(packed_ref.at[c], out_ref.at[pl.ds(c * share, share)], out_sems.at[c])
        )
        results[-1].start()
    for result in results:
        result.wait()


def fold_kernel(wanted_ref, replies_ref, out_ref):
    group, rows, width = replies_ref.shape
    picks = slots_of(wanted_ref, 1, rows, out_ref.shape[1])
    out_ref[...] = dot(replies_ref[...].reshape(group * rows, width), picks, 0, 0).astype(jnp.bfloat16)


def keep_kernel(in_ref, out_ref):
    pass


def finish_kernel(wanted_ref, replies_ref, out_ref):
    group, rows, width = replies_ref.shape
    picks = slots_of(wanted_ref, 0, rows, out_ref.shape[1])
    out_ref[...] = dot(replies_ref[...].reshape(group * rows, width), picks, 0, 0)


def attend_kernel(
    windows,
    codes_ref,
    own_ref,
    other_ref,
    out_own_ref,
    out_other_ref,
    feats_ref,
    grads_ref,
    scores_ref,
    dprobs_ref,
    probs_ref,
    dscores_ref,
    falls_ref,
):
    group, rows, width4 = own_ref.shape
    feat = width4 // 4
    head_dim = feat // HEADS
    scale = head_dim**-0.5
    tables, points = codes_ref.shape
    buckets = points // BUCKET
    pair = 2 * head_dim
    bf16 = jnp.bfloat16
    head_of = lax.broadcasted_iota(jnp.int32, (pair, 2 * BUCKET), 0) // head_dim
    block_of = lax.broadcasted_iota(jnp.int32, (pair, 2 * BUCKET), 1) // BUCKET
    mask = jnp.where(head_of == block_of, 1.0, 0.0).astype(bf16)
    tail = lax.broadcasted_iota(jnp.int32, (16, BUCKET), 0)
    tail_wide = lax.broadcasted_iota(jnp.int32, (16, 2 * BUCKET), 0)
    tail_block = lax.broadcasted_iota(jnp.int32, (16, 2 * BUCKET), 1) // BUCKET
    halves = jnp.where((tail_wide < 6) & (tail_wide // 3 == tail_block), -0.5, 0.0).astype(bf16)
    lane = lax.broadcasted_iota(jnp.int32, (BUCKET, BUCKET), 1)

    def blocked(part):
        return jnp.concatenate([part, part], axis=1) * mask

    def norm_rows(k):
        wide = k.astype(jnp.float32)
        squares = wide * wide
        first, second = (
            jnp.sum(squares[i * head_dim : (i + 1) * head_dim], axis=0, keepdims=True) for i in range(2)
        )
        norm = jnp.where(tail < 3, first, second)
        high = norm.astype(bf16).astype(jnp.float32)
        rest = norm - high
        middle = rest.astype(bf16).astype(jnp.float32)
        piece = tail % 3
        out = jnp.where(piece == 0, high, jnp.where(piece == 1, middle, rest - middle))
        return jnp.where(tail < 6, out, 0.0).astype(bf16)

    out_own_ref[...] = jnp.zeros_like(out_own_ref)
    out_other_ref[...] = jnp.zeros_like(out_other_ref)
    todo = [(b, h) for b in range(buckets) for h in range(HEADS // 2)]
    for t in range(tables):
        low, high = windows[t]
        span = high - low
        slots = 2 * group * span
        codes = codes_ref[t : t + 1, :].astype(jnp.float32)
        places = lax.broadcasted_iota(jnp.int32, (slots, points), 0).astype(jnp.float32)
        picks = jnp.where(places == codes, 1.0, 0.0).astype(bf16)
        arrived = jnp.concatenate(
            [ref[:, low:high, :].reshape(group * span, width4) for ref in (own_ref, other_ref)], axis=0
        )
        feats_ref[...] = dot(arrived, picks, 0, 0).astype(bf16)

        def part_of(which, b, h):
            at = which * feat + h * pair
            return feats_ref[at : at + pair, b * BUCKET : (b + 1) * BUCKET]

        for n, (b, h) in enumerate(todo):
            q, k, v, g = (part_of(which, b, h) for which in range(4))
            scores_ref[n] = dot(
                jnp.concatenate([k, norm_rows(k)], axis=0), jnp.concatenate([blocked(q), halves], axis=0), 0, 0
            )
            dprobs_ref[n] = dot(v, blocked(g), 0, 0)
        for n in range(len(todo)):
            for i in range(2):
                cols = slice(i * BUCKET, (i + 1) * BUCKET)
                dprob = dprobs_ref[n, :, cols]
                scores = scores_ref[n, :, cols]
                expons = jnp.exp2((scores - jnp.max(scores, axis=0, keepdims=True)) * (scale * LOG2E))
                probs = expons * (1.0 / jnp.sum(expons, axis=0, keepdims=True))
                delta = jnp.sum(probs * dprob, axis=0, keepdims=True)
                dscore = probs * (dprob - delta)
                probs_ref[n, :, cols] = probs.astype(bf16)
                dscores_ref[n, :, cols] = dscore.astype(bf16)
                falls_ref[n, i] = jnp.broadcast_to(jnp.sum(dscore, axis=1, keepdims=True), (BUCKET, BUCKET))
        for n, (b, h) in enumerate(todo):
            if h == 0:
                falls = sum(
                    jnp.where(lane == i, falls_ref[b * (HEADS // 2) + i // 2, i % 2], 0.0) for i in range(HEADS)
                ).T
            q, k, g = (part_of(which, b, h) for which in (0, 1, 3))
            dscore_tall = jnp.concatenate([dscores_ref[n, :, :BUCKET], dscores_ref[n, :, BUCKET:]], axis=0)
            dq = scale * dot(blocked(k), dscore_tall, 1, 0)
            fall = jnp.concatenate(
                [jnp.broadcast_to(falls[i : i + 1], (head_dim, BUCKET)) for i in (2 * h, 2 * h + 1)], axis=0
            )
            dk = scale * (dot(blocked(q), dscores_ref[n], 1, 1) - fall * k.astype(jnp.float32))
            dv = dot(blocked(g), probs_ref[n], 1, 1)
            for which, grad in enumerate((dq, dk, dv)):
                at = which * feat + h * pair
                grads_ref[at : at + pair, b * BUCKET : (b + 1) * BUCKET] = grad.astype(bf16)
        back = dot(picks, grads_ref[...], 1, 1).astype(bf16).reshape(2, group, span, 3 * feat)
        for part, ref in enumerate((out_own_ref, out_other_ref)):
            ref[:, low:high, :] = ref[:, low:high, :] + back[part]


def call(kernel, out_shape, scratch=(), flops=0, moved=0, in_specs=None, out_specs=None, vmem_bytes=VMEM_BYTES):
    extra = {name: specs for name, specs in (("in_specs", in_specs), ("out_specs", out_specs)) if specs is not None}
    return pl.pallas_call(
        kernel,
        out_shape=out_shape,
        scratch_shapes=list(scratch),
        compiler_params=pltpu.CompilerParams(vmem_limit_bytes=vmem_bytes),
        cost_estimate=pl.CostEstimate(flops=flops, bytes_accessed=moved, transcendentals=0),
        **extra,
    )


def on_device(query, key_rows, value, out_grad, members):
    feat, points = query.shape
    tables = members.shape[0]
    phi, eta = lax.axis_size("phi"), lax.axis_size("eta")
    half = eta // 2
    group = phi * half
    capacity = 5 * points // (4 * phi * eta)
    rows = -(-tables * capacity // 16) * 16
    windows = [(t * capacity // 16 * 16, -(-(t * capacity + capacity) // 16) * 16) for t in range(tables)]
    halves = [[p * eta + h * half + e for p in range(phi) for e in range(half)] for h in range(2)]
    layer = eta // 4
    across = [
        (p * eta + z * layer + e, p * eta + (3 - z) * layer + e) for p in range(phi) for z in range(4) for e in range(layer)
    ]
    bf16 = jnp.bfloat16
    packed = jax.ShapeDtypeStruct((group, rows, 4 * feat), bf16)
    reply = jax.ShapeDtypeStruct((group, rows, 3 * feat), bf16)
    steps = points // BUCKET * (HEADS // 2)
    vmem, hbm = pl.BlockSpec(memory_space=pltpu.VMEM), pl.BlockSpec(memory_space=pl.ANY)

    def exchange(chunks):
        return lax.all_to_all(chunks, AXES, 0, 0, tiled=True, axis_index_groups=halves)

    def pack(part, flops):
        return call(
            functools.partial(pack_kernel, part),
            packed,
            scratch=(
                pltpu.VMEM((4 * feat, points), bf16),
                pltpu.VMEM((PACK_STEPS, group // PACK_STEPS, rows, 4 * feat), bf16),
                pltpu.SemaphoreType.DMA((4,)),
                pltpu.SemaphoreType.DMA((PACK_STEPS,)),
            ),
            out_specs=pl.BlockSpec(memory_space=pl.ANY),
            in_specs=[vmem] + [pl.BlockSpec(memory_space=pltpu.HBM)] * 4,
            flops=flops,
            moved=2 * group * rows * 4 * feat,
            vmem_bytes=WHOLE_VMEM_BYTES if part else VMEM_BYTES,
        )

    arrays = (query, key_rows, value, out_grad)
    copies = [lax.ppermute(array, AXES, across) for array in arrays]

    index = call(
        functools.partial(index_kernel, (windows, capacity, rows, eta)),
        (
            jax.ShapeDtypeStruct((group, 8, 2 * rows), jnp.int32),
            jax.ShapeDtypeStruct((tables, points), jnp.int32),
        ),
        in_specs=[pl.BlockSpec(memory_space=pltpu.SMEM), vmem],
        flops=10**9,
        moved=10**5,
    )
    wanted, codes = index((lax.axis_index("eta") // half).astype(jnp.int32).reshape(1, 1), members)
    wanted = exchange(wanted)

    arrived_own = exchange(pack(0, 2 * group * rows * points * 4 * feat)(wanted, *arrays))
    arrived_other = exchange(pack(1, PACK_FLOPS)(wanted, *copies))
    attend = call(
        functools.partial(attend_kernel, windows),
        (reply, reply),
        scratch=(
            pltpu.VMEM((4 * feat, points), bf16),
            pltpu.VMEM((3 * feat, points), bf16),
            pltpu.VMEM((steps, BUCKET, 2 * BUCKET), jnp.float32),
            pltpu.VMEM((steps, BUCKET, 2 * BUCKET), jnp.float32),
            pltpu.VMEM((steps, BUCKET, 2 * BUCKET), bf16),
            pltpu.VMEM((steps, BUCKET, 2 * BUCKET), bf16),
            pltpu.VMEM((steps, 2, BUCKET, BUCKET), jnp.float32),
        ),
        flops=2 * 10**10,
        moved=8 * 10**6,
    )
    reply_own, reply_other = attend(codes, arrived_own, arrived_other)
    returned_other = exchange(reply_other)
    fold = call(
        fold_kernel,
        jax.ShapeDtypeStruct((3 * feat, points), bf16),
        flops=2 * group * rows * points * 3 * feat,
        moved=2 * group * rows * 3 * feat,
    )
    folded, reply_own = lax.optimization_barrier((fold(wanted, returned_other), reply_own))
    summed = lax.ppermute(folded, AXES, across)
    summed = pl.pallas_call(
        keep_kernel,
        out_shape=jax.ShapeDtypeStruct((3 * feat, points), bf16),
        in_specs=[hbm],
        out_specs=hbm,
        input_output_aliases={0: 0},
        cost_estimate=pl.CostEstimate(flops=PACK_FLOPS, bytes_accessed=0, transcendentals=0),
    )(summed)
    returned_own = exchange(reply_own)
    finish = call(
        finish_kernel,
        jax.ShapeDtypeStruct((3 * feat, points), jnp.float32),
        flops=2 * group * rows * points * 3 * feat,
        moved=2 * group * rows * 3 * feat,
    )
    total = (finish(wanted, returned_own) + summed.astype(jnp.float32)).astype(bf16)
    return total[:feat], total[feat : 2 * feat], total[2 * feat :]


def solution(mesh):
    split = P(None, AXES)
    in_specs = (split, split, split, split, P(None, AXES, None))
    return jax.shard_map(
        on_device, mesh=mesh, in_specs=in_specs, out_specs=(split, split, split), check_vma=False
    )
```

```python
import functools

import jax
import jax.numpy as jnp
from jax import lax
from jax.experimental import pallas as pl
from jax.experimental.pallas import tpu as pltpu
from jax.sharding import PartitionSpec as P

HEADS = 8
BUCKET = 128
AXES = ("phi", "eta")
LOG2E = 1.4426950408889634
VMEM_BYTES = 48 * 1024 * 1024
WHOLE_VMEM_BYTES = 62 * 1024 * 1024
PACK_FLOPS = 4 * 10**10
PACK_STEPS = 4


def dot(a, b, da, db):
    return lax.dot_general(a, b, (((da,), (db,)), ((), ())), preferred_element_type=jnp.float32)


def column_of(row, first, count):
    n = row.shape[1]
    diagonal = lax.broadcasted_iota(jnp.int32, (count, n), 0) + first == lax.broadcasted_iota(jnp.int32, (count, n), 1)
    return jnp.sum(jnp.where(diagonal, jnp.broadcast_to(row, (count, n)), 0.0), axis=1, keepdims=True)


def slots_of(wanted_ref, part, rows, points, owners=None):
    places = lax.broadcasted_iota(jnp.int32, (rows, points), 1).astype(jnp.float32)
    picks = []
    for o in range(wanted_ref.shape[0]) if owners is None else owners:
        wanted = wanted_ref[o, :1].astype(jnp.float32)
        picks.append(jnp.where(column_of(wanted, part * rows, rows) == places, 1.0, 0.0).astype(jnp.bfloat16))
    return jnp.concatenate(picks, axis=0)


def index_kernel(sizes, half_ref, members_ref, wanted_ref, codes_ref):
    windows, capacity, rows, eta = sizes
    tables, buckets, _ = members_ref.shape
    points = buckets * BUCKET
    group = wanted_ref.shape[0]
    half = eta // 2
    f32, bf16 = jnp.float32, jnp.bfloat16
    ids = jnp.concatenate([members_ref[:, b, :] for b in range(buckets)], axis=1).astype(f32)
    home = jnp.floor((ids + 0.5) * (1.0 / points))
    local = ids - home * points
    home_p = jnp.floor((home + 0.5) * (1.0 / eta))
    home_e = home - home_p * eta
    home_h = jnp.floor((home_e + 0.5) * (1.0 / half))
    part = jnp.where(home_h == half_ref[0, 0].astype(f32), 0.0, 1.0)
    within = home_e - home_h * half
    deep = jnp.floor((within + 0.5) * (2.0 / half))
    place = home_p * half + within + part * (0.5 * half) * (1.0 - 2.0 * deep)
    before = lax.broadcasted_iota(jnp.int32, (points, points), 0) < lax.broadcasted_iota(jnp.int32, (points, points), 1)
    before = jnp.where(before, 1.0, 0.0).astype(bf16)
    homes = lax.broadcasted_iota(jnp.int32, (2 * group, points), 0).astype(f32)
    holders = lax.broadcasted_iota(jnp.int32, (group, points), 0).astype(f32)
    lanes = lax.broadcasted_iota(jnp.int32, (2 * rows, points), 0).astype(f32)
    total = jnp.zeros((2 * group, 2 * rows), f32)
    for t in range(tables):
        row = slice(t, t + 1)
        hot = jnp.where(homes == home[row], 1.0, 0.0)
        rank = jnp.sum(hot * dot(hot.astype(bf16), before, 1, 0), axis=0, keepdims=True)
        slot = rank + float(t * capacity)
        low, high = windows[t]
        code = (part[row] * float(group) + place[row]) * float(high - low) + slot - float(low)
        codes_ref[row, :] = code.astype(jnp.int32)
        named = local[row] + 1.0
        large = jnp.floor(named * (1.0 / 256.0)) * 256.0
        held = holders == place[row]
        values = jnp.concatenate([jnp.where(held, large, 0.0), jnp.where(held, named - large, 0.0)], axis=0)
        at = jnp.where(lanes == part[row] * float(rows) + slot, 1.0, 0.0)
        total += dot(values.astype(bf16), at.astype(bf16), 1, 1)
    wanted = (total[:group] + total[group:] - 1.0).astype(jnp.int32)
    for o in range(group):
        wanted_ref[o] = jnp.broadcast_to(wanted[o : o + 1], wanted_ref.shape[1:])


def pack_kernel(part, wanted_ref, q_ref, k_ref, v_ref, g_ref, out_ref, features_ref, packed_ref, sems, out_sems):
    group, rows, width = out_ref.shape
    feat, points = q_ref.shape
    copies = [
        pltpu.make_async_copy(ref, features_ref.at[pl.ds(n * feat, feat)], sems.at[n])
        for n, ref in enumerate((q_ref, k_ref, v_ref, g_ref))
    ]
    for copy in copies:
        copy.start()
    share = group // PACK_STEPS
    picks = [
        slots_of(wanted_ref, part, rows, points, range(c * share, (c + 1) * share)) for c in range(PACK_STEPS)
    ]
    for copy in copies:
        copy.wait()
    features = features_ref[...]
    results = []
    for c in range(PACK_STEPS):
        packed = dot(picks[c], features, 1, 1).astype(jnp.bfloat16)
        packed_ref[c] = packed.reshape(share, rows, width)
        results.append(
            pltpu.make_async_copy(packed_ref.at[c], out_ref.at[pl.ds(c * share, share)], out_sems.at[c])
        )
        results[-1].start()
    for result in results:
        result.wait()


def fold_kernel(wanted_ref, replies_ref, out_ref):
    group, rows, width = replies_ref.shape
    picks = slots_of(wanted_ref, 1, rows, out_ref.shape[1])
    out_ref[...] = dot(replies_ref[...].reshape(group * rows, width), picks, 0, 0).astype(jnp.bfloat16)


def keep_kernel(in_ref, out_ref):
    pass


def finish_kernel(wanted_ref, replies_ref, q_ref, k_ref, v_ref):
    group, rows, width = replies_ref.shape
    feat, points = q_ref.shape
    picks = slots_of(wanted_ref, 0, rows, points)
    total = dot(replies_ref[...].reshape(group * rows, width), picks, 0, 0)
    for n, ref in enumerate((q_ref, k_ref, v_ref)):
        ref[...] = total[n * feat : (n + 1) * feat]


def attend_kernel(
    windows,
    codes_ref,
    own_ref,
    other_ref,
    out_own_ref,
    out_other_ref,
    feats_ref,
    grads_ref,
    scores_ref,
    dprobs_ref,
    probs_ref,
    dscores_ref,
    falls_ref,
):
    group, rows, width4 = own_ref.shape
    feat = width4 // 4
    head_dim = feat // HEADS
    scale = head_dim**-0.5
    tables, points = codes_ref.shape
    buckets = points // BUCKET
    pair = 2 * head_dim
    bf16 = jnp.bfloat16
    head_of = lax.broadcasted_iota(jnp.int32, (pair, 2 * BUCKET), 0) // head_dim
    block_of = lax.broadcasted_iota(jnp.int32, (pair, 2 * BUCKET), 1) // BUCKET
    mask = jnp.where(head_of == block_of, 1.0, 0.0).astype(bf16)
    tail = lax.broadcasted_iota(jnp.int32, (16, BUCKET), 0)
    tail_wide = lax.broadcasted_iota(jnp.int32, (16, 2 * BUCKET), 0)
    tail_block = lax.broadcasted_iota(jnp.int32, (16, 2 * BUCKET), 1) // BUCKET
    halves = jnp.where((tail_wide < 6) & (tail_wide // 3 == tail_block), -0.5, 0.0).astype(bf16)
    lane = lax.broadcasted_iota(jnp.int32, (BUCKET, BUCKET), 1)

    def blocked(part):
        return jnp.concatenate([part, part], axis=1) * mask

    def norm_rows(k):
        wide = k.astype(jnp.float32)
        squares = wide * wide
        first, second = (
            jnp.sum(squares[i * head_dim : (i + 1) * head_dim], axis=0, keepdims=True) for i in range(2)
        )
        norm = jnp.where(tail < 3, first, second)
        high = norm.astype(bf16).astype(jnp.float32)
        rest = norm - high
        middle = rest.astype(bf16).astype(jnp.float32)
        piece = tail % 3
        out = jnp.where(piece == 0, high, jnp.where(piece == 1, middle, rest - middle))
        return jnp.where(tail < 6, out, 0.0).astype(bf16)

    out_own_ref[...] = jnp.zeros_like(out_own_ref)
    out_other_ref[...] = jnp.zeros_like(out_other_ref)
    todo = [(b, h) for b in range(buckets) for h in range(HEADS // 2)]
    for t in range(tables):
        low, high = windows[t]
        span = high - low
        slots = 2 * group * span
        codes = codes_ref[t : t + 1, :].astype(jnp.float32)
        places = lax.broadcasted_iota(jnp.int32, (slots, points), 0).astype(jnp.float32)
        picks = jnp.where(places == codes, 1.0, 0.0).astype(bf16)
        arrived = jnp.concatenate(
            [ref[:, low:high, :].reshape(group * span, width4) for ref in (own_ref, other_ref)], axis=0
        )
        feats_ref[...] = dot(arrived, picks, 0, 0).astype(bf16)

        def part_of(which, b, h):
            at = which * feat + h * pair
            return feats_ref[at : at + pair, b * BUCKET : (b + 1) * BUCKET]

        for n, (b, h) in enumerate(todo):
            q, k, v, g = (part_of(which, b, h) for which in range(4))
            scores_ref[n] = dot(
                jnp.concatenate([k, norm_rows(k)], axis=0), jnp.concatenate([blocked(q), halves], axis=0), 0, 0
            )
            dprobs_ref[n] = dot(v, blocked(g), 0, 0)
        for n in range(len(todo)):
            for i in range(2):
                cols = slice(i * BUCKET, (i + 1) * BUCKET)
                dprob = dprobs_ref[n, :, cols]
                scores = scores_ref[n, :, cols]
                expons = jnp.exp2((scores - jnp.max(scores, axis=0, keepdims=True)) * (scale * LOG2E))
                probs = expons * (1.0 / jnp.sum(expons, axis=0, keepdims=True))
                delta = jnp.sum(probs * dprob, axis=0, keepdims=True)
                dscore = probs * (dprob - delta)
                probs_ref[n, :, cols] = probs.astype(bf16)
                dscores_ref[n, :, cols] = dscore.astype(bf16)
                falls_ref[n, i] = jnp.broadcast_to(jnp.sum(dscore, axis=1, keepdims=True), (BUCKET, BUCKET))
        for n, (b, h) in enumerate(todo):
            if h == 0:
                falls = sum(
                    jnp.where(lane == i, falls_ref[b * (HEADS // 2) + i // 2, i % 2], 0.0) for i in range(HEADS)
                ).T
            q, k, g = (part_of(which, b, h) for which in (0, 1, 3))
            dscore_tall = jnp.concatenate([dscores_ref[n, :, :BUCKET], dscores_ref[n, :, BUCKET:]], axis=0)
            dq = scale * dot(blocked(k), dscore_tall, 1, 0)
            fall = jnp.concatenate(
                [jnp.broadcast_to(falls[i : i + 1], (head_dim, BUCKET)) for i in (2 * h, 2 * h + 1)], axis=0
            )
            dk = scale * (dot(blocked(q), dscores_ref[n], 1, 1) - fall * k.astype(jnp.float32))
            dv = dot(blocked(g), probs_ref[n], 1, 1)
            for which, grad in enumerate((dq, dk, dv)):
                at = which * feat + h * pair
                grads_ref[at : at + pair, b * BUCKET : (b + 1) * BUCKET] = grad.astype(bf16)
        back = dot(picks, grads_ref[...], 1, 1).astype(bf16).reshape(2, group, span, 3 * feat)
        for part, ref in enumerate((out_own_ref, out_other_ref)):
            ref[:, low:high, :] = ref[:, low:high, :] + back[part]


def call(kernel, out_shape, scratch=(), flops=0, moved=0, in_specs=None, out_specs=None, vmem_bytes=VMEM_BYTES):
    extra = {name: specs for name, specs in (("in_specs", in_specs), ("out_specs", out_specs)) if specs is not None}
    return pl.pallas_call(
        kernel,
        out_shape=out_shape,
        scratch_shapes=list(scratch),
        compiler_params=pltpu.CompilerParams(vmem_limit_bytes=vmem_bytes),
        cost_estimate=pl.CostEstimate(flops=flops, bytes_accessed=moved, transcendentals=0),
        **extra,
    )


def on_device(query, key_rows, value, out_grad, members):
    feat, points = query.shape
    tables = members.shape[0]
    phi, eta = lax.axis_size("phi"), lax.axis_size("eta")
    half = eta // 2
    group = phi * half
    capacity = 5 * points // (4 * phi * eta)
    rows = -(-tables * capacity // 16) * 16
    windows = [(t * capacity // 16 * 16, -(-(t * capacity + capacity) // 16) * 16) for t in range(tables)]
    halves = [[p * eta + h * half + e for p in range(phi) for e in range(half)] for h in range(2)]
    layer = eta // 4
    across = [
        (p * eta + z * layer + e, p * eta + (3 - z) * layer + e) for p in range(phi) for z in range(4) for e in range(layer)
    ]
    bf16 = jnp.bfloat16
    packed = jax.ShapeDtypeStruct((group, rows, 4 * feat), bf16)
    reply = jax.ShapeDtypeStruct((group, rows, 3 * feat), bf16)
    steps = points // BUCKET * (HEADS // 2)
    vmem, hbm = pl.BlockSpec(memory_space=pltpu.VMEM), pl.BlockSpec(memory_space=pl.ANY)

    def exchange(chunks):
        return lax.all_to_all(chunks, AXES, 0, 0, tiled=True, axis_index_groups=halves)

    def pack(part, flops):
        return call(
            functools.partial(pack_kernel, part),
            packed,
            scratch=(
                pltpu.VMEM((4 * feat, points), bf16),
                pltpu.VMEM((PACK_STEPS, group // PACK_STEPS, rows, 4 * feat), bf16),
                pltpu.SemaphoreType.DMA((4,)),
                pltpu.SemaphoreType.DMA((PACK_STEPS,)),
            ),
            out_specs=pl.BlockSpec(memory_space=pl.ANY),
            in_specs=[vmem] + [pl.BlockSpec(memory_space=pltpu.HBM)] * 4,
            flops=flops,
            moved=2 * group * rows * 4 * feat,
            vmem_bytes=WHOLE_VMEM_BYTES,
        )

    arrays = (query, key_rows, value, out_grad)
    copies = [lax.ppermute(array, AXES, across) for array in arrays]

    index = call(
        functools.partial(index_kernel, (windows, capacity, rows, eta)),
        (
            jax.ShapeDtypeStruct((group, 8, 2 * rows), jnp.int32),
            jax.ShapeDtypeStruct((tables, points), jnp.int32),
        ),
        in_specs=[pl.BlockSpec(memory_space=pltpu.SMEM), vmem],
        flops=10**9,
        moved=10**5,
    )
    wanted, codes = index((lax.axis_index("eta") // half).astype(jnp.int32).reshape(1, 1), members)
    wanted = exchange(wanted)

    arrived_own = exchange(pack(0, 2 * group * rows * points * 4 * feat)(wanted, *arrays))
    arrived_other = exchange(pack(1, PACK_FLOPS)(wanted, *copies))
    attend = call(
        functools.partial(attend_kernel, windows),
        (reply, reply),
        scratch=(
            pltpu.VMEM((4 * feat, points), bf16),
            pltpu.VMEM((3 * feat, points), bf16),
            pltpu.VMEM((steps, BUCKET, 2 * BUCKET), jnp.float32),
            pltpu.VMEM((steps, BUCKET, 2 * BUCKET), jnp.float32),
            pltpu.VMEM((steps, BUCKET, 2 * BUCKET), bf16),
            pltpu.VMEM((steps, BUCKET, 2 * BUCKET), bf16),
            pltpu.VMEM((steps, 2, BUCKET, BUCKET), jnp.float32),
        ),
        flops=2 * 10**10,
        moved=8 * 10**6,
    )
    reply_own, reply_other = attend(codes, arrived_own, arrived_other)
    returned_other = exchange(reply_other)
    fold = call(
        fold_kernel,
        jax.ShapeDtypeStruct((3 * feat, points), bf16),
        flops=2 * group * rows * points * 3 * feat,
        moved=2 * group * rows * 3 * feat,
    )
    folded, reply_own = lax.optimization_barrier((fold(wanted, returned_other), reply_own))
    summed = lax.ppermute(folded, AXES, across)
    summed = pl.pallas_call(
        keep_kernel,
        out_shape=jax.ShapeDtypeStruct((3 * feat, points), bf16),
        in_specs=[hbm],
        out_specs=hbm,
        input_output_aliases={0: 0},
        cost_estimate=pl.CostEstimate(flops=PACK_FLOPS, bytes_accessed=0, transcendentals=0),
    )(summed)
    returned_own = exchange(reply_own)
    finish = call(
        finish_kernel,
        (jax.ShapeDtypeStruct((feat, points), jnp.float32),) * 3,
        flops=2 * group * rows * points * 3 * feat,
        moved=2 * group * rows * 3 * feat,
    )
    own_sums = finish(wanted, returned_own)
    return tuple(
        (own + summed[n * feat : (n + 1) * feat].astype(jnp.float32)).astype(bf16) for n, own in enumerate(own_sums)
    )


def solution(mesh):
    split = P(None, AXES)
    in_specs = (split, split, split, split, P(None, AXES, None))
    return jax.shard_map(
        on_device, mesh=mesh, in_specs=in_specs, out_specs=(split, split, split), check_vma=False
    )
```

```python
import functools

import jax
import jax.numpy as jnp
from jax import lax
from jax.experimental import pallas as pl
from jax.experimental.pallas import tpu as pltpu
from jax.sharding import PartitionSpec as P

HEADS = 8
BUCKET = 128
AXES = ("phi", "eta")
LOG2E = 1.4426950408889634
VMEM_BYTES = 48 * 1024 * 1024
WHOLE_VMEM_BYTES = 62 * 1024 * 1024
PACK_FLOPS = 4 * 10**10
PACK_STEPS = 4


def dot(a, b, da, db):
    return lax.dot_general(a, b, (((da,), (db,)), ((), ())), preferred_element_type=jnp.float32)


def column_of(row, first, count):
    n = row.shape[1]
    diagonal = lax.broadcasted_iota(jnp.int32, (count, n), 0) + first == lax.broadcasted_iota(jnp.int32, (count, n), 1)
    return jnp.sum(jnp.where(diagonal, jnp.broadcast_to(row, (count, n)), 0.0), axis=1, keepdims=True)


def slots_of(wanted_ref, part, rows, points, owners=None):
    places = lax.broadcasted_iota(jnp.int32, (rows, points), 1).astype(jnp.float32)
    picks = []
    for o in range(wanted_ref.shape[0]) if owners is None else owners:
        wanted = wanted_ref[o, :1].astype(jnp.float32)
        picks.append(jnp.where(column_of(wanted, part * rows, rows) == places, 1.0, 0.0).astype(jnp.bfloat16))
    return jnp.concatenate(picks, axis=0)


def index_kernel(sizes, half_ref, members_ref, wanted_ref, codes_ref):
    windows, capacity, rows, eta = sizes
    tables, buckets, _ = members_ref.shape
    points = buckets * BUCKET
    group = wanted_ref.shape[0]
    half = eta // 2
    f32, bf16 = jnp.float32, jnp.bfloat16
    ids = jnp.concatenate([members_ref[:, b, :] for b in range(buckets)], axis=1).astype(f32)
    home = jnp.floor((ids + 0.5) * (1.0 / points))
    local = ids - home * points
    home_p = jnp.floor((home + 0.5) * (1.0 / eta))
    home_e = home - home_p * eta
    home_h = jnp.floor((home_e + 0.5) * (1.0 / half))
    part = jnp.where(home_h == half_ref[0, 0].astype(f32), 0.0, 1.0)
    within = home_e - home_h * half
    deep = jnp.floor((within + 0.5) * (2.0 / half))
    place = home_p * half + within + part * (0.5 * half) * (1.0 - 2.0 * deep)
    before = lax.broadcasted_iota(jnp.int32, (points, points), 0) < lax.broadcasted_iota(jnp.int32, (points, points), 1)
    before = jnp.where(before, 1.0, 0.0).astype(bf16)
    homes = lax.broadcasted_iota(jnp.int32, (2 * group, points), 0).astype(f32)
    holders = lax.broadcasted_iota(jnp.int32, (group, points), 0).astype(f32)
    lanes = lax.broadcasted_iota(jnp.int32, (2 * rows, points), 0).astype(f32)
    total = jnp.zeros((2 * group, 2 * rows), f32)
    for t in range(tables):
        row = slice(t, t + 1)
        hot = jnp.where(homes == home[row], 1.0, 0.0)
        rank = jnp.sum(hot * dot(hot.astype(bf16), before, 1, 0), axis=0, keepdims=True)
        slot = rank + float(t * capacity)
        low, high = windows[t]
        code = (part[row] * float(group) + place[row]) * float(high - low) + slot - float(low)
        codes_ref[row, :] = code.astype(jnp.int32)
        named = local[row] + 1.0
        large = jnp.floor(named * (1.0 / 256.0)) * 256.0
        held = holders == place[row]
        values = jnp.concatenate([jnp.where(held, large, 0.0), jnp.where(held, named - large, 0.0)], axis=0)
        at = jnp.where(lanes == part[row] * float(rows) + slot, 1.0, 0.0)
        total += dot(values.astype(bf16), at.astype(bf16), 1, 1)
    wanted = (total[:group] + total[group:] - 1.0).astype(jnp.int32)
    for o in range(group):
        wanted_ref[o] = jnp.broadcast_to(wanted[o : o + 1], wanted_ref.shape[1:])


def pack_kernel(part, wanted_ref, q_ref, k_ref, v_ref, g_ref, out_ref, features_ref, packed_ref, sems, out_sems):
    group, rows, width = out_ref.shape
    feat, points = q_ref.shape
    copies = [
        pltpu.make_async_copy(ref, features_ref.at[pl.ds(n * feat, feat)], sems.at[n])
        for n, ref in enumerate((q_ref, k_ref, v_ref, g_ref))
    ]
    for copy in copies:
        copy.start()
    share = group // PACK_STEPS
    picks = [
        slots_of(wanted_ref, part, rows, points, range(c * share, (c + 1) * share)) for c in range(PACK_STEPS)
    ]
    for copy in copies:
        copy.wait()
    features = features_ref[...]
    results = []
    for c in range(PACK_STEPS):
        packed = dot(picks[c], features, 1, 1).astype(jnp.bfloat16)
        packed_ref[c] = packed.reshape(share, rows, width)
        results.append(
            pltpu.make_async_copy(packed_ref.at[c], out_ref.at[pl.ds(c * share, share)], out_sems.at[c])
        )
        results[-1].start()
    for result in results:
        result.wait()


def fold_kernel(wanted_ref, replies_ref, out_ref):
    group, rows, width = replies_ref.shape
    picks = slots_of(wanted_ref, 1, rows, out_ref.shape[1])
    out_ref[...] = dot(replies_ref[...].reshape(group * rows, width), picks, 0, 0).astype(jnp.bfloat16)


def keep_kernel(in_ref, out_ref):
    pass


def finish_kernel(wanted_ref, replies_ref, q_ref, k_ref, v_ref):
    group, rows, width = replies_ref.shape
    feat, points = q_ref.shape
    picks = slots_of(wanted_ref, 0, rows, points)
    total = dot(replies_ref[...].reshape(group * rows, width), picks, 0, 0)
    for n, ref in enumerate((q_ref, k_ref, v_ref)):
        ref[...] = total[n * feat : (n + 1) * feat]


def attend_kernel(
    windows,
    codes_ref,
    own_ref,
    other_ref,
    out_own_ref,
    out_other_ref,
    feats_ref,
    grads_ref,
    scores_ref,
    dprobs_ref,
    probs_ref,
    dscores_ref,
    falls_ref,
):
    group, rows, width4 = own_ref.shape
    feat = width4 // 4
    head_dim = feat // HEADS
    scale = head_dim**-0.5
    tables, points = codes_ref.shape
    buckets = points // BUCKET
    pair = 2 * head_dim
    bf16 = jnp.bfloat16
    head_of = lax.broadcasted_iota(jnp.int32, (pair, 2 * BUCKET), 0) // head_dim
    block_of = lax.broadcasted_iota(jnp.int32, (pair, 2 * BUCKET), 1) // BUCKET
    mask = jnp.where(head_of == block_of, 1.0, 0.0).astype(bf16)
    tail = lax.broadcasted_iota(jnp.int32, (16, BUCKET), 0)
    tail_wide = lax.broadcasted_iota(jnp.int32, (16, 2 * BUCKET), 0)
    tail_block = lax.broadcasted_iota(jnp.int32, (16, 2 * BUCKET), 1) // BUCKET
    halves = jnp.where((tail_wide < 6) & (tail_wide // 3 == tail_block), -0.5, 0.0).astype(bf16)
    lane = lax.broadcasted_iota(jnp.int32, (BUCKET, BUCKET), 1)

    def blocked(part):
        return jnp.concatenate([part, part], axis=1) * mask

    def norm_rows(k):
        wide = k.astype(jnp.float32)
        squares = wide * wide
        first, second = (
            jnp.sum(squares[i * head_dim : (i + 1) * head_dim], axis=0, keepdims=True) for i in range(2)
        )
        norm = jnp.where(tail < 3, first, second)
        high = norm.astype(bf16).astype(jnp.float32)
        rest = norm - high
        middle = rest.astype(bf16).astype(jnp.float32)
        piece = tail % 3
        out = jnp.where(piece == 0, high, jnp.where(piece == 1, middle, rest - middle))
        return jnp.where(tail < 6, out, 0.0).astype(bf16)

    out_own_ref[...] = jnp.zeros_like(out_own_ref)
    out_other_ref[...] = jnp.zeros_like(out_other_ref)
    todo = [(b, h) for b in range(buckets) for h in range(HEADS // 2)]
    for t in range(tables):
        low, high = windows[t]
        span = high - low
        slots = 2 * group * span
        codes = codes_ref[t : t + 1, :].astype(jnp.float32)
        places = lax.broadcasted_iota(jnp.int32, (slots, points), 0).astype(jnp.float32)
        picks = jnp.where(places == codes, 1.0, 0.0).astype(bf16)
        arrived = jnp.concatenate(
            [ref[:, low:high, :].reshape(group * span, width4) for ref in (own_ref, other_ref)], axis=0
        )
        feats_ref[...] = dot(arrived, picks, 0, 0).astype(bf16)

        def part_of(which, b, h):
            at = which * feat + h * pair
            return feats_ref[at : at + pair, b * BUCKET : (b + 1) * BUCKET]

        for n, (b, h) in enumerate(todo):
            q, k, v, g = (part_of(which, b, h) for which in range(4))
            scores_ref[n] = dot(
                jnp.concatenate([k, norm_rows(k)], axis=0), jnp.concatenate([blocked(q), halves], axis=0), 0, 0
            )
            dprobs_ref[n] = dot(v, blocked(g), 0, 0)
        for n in range(len(todo)):
            for i in range(2):
                cols = slice(i * BUCKET, (i + 1) * BUCKET)
                dprob = dprobs_ref[n, :, cols]
                scores = scores_ref[n, :, cols]
                expons = jnp.exp2((scores - jnp.max(scores, axis=0, keepdims=True)) * (scale * LOG2E))
                probs = expons * (1.0 / jnp.sum(expons, axis=0, keepdims=True))
                probs_low = probs.astype(bf16)
                delta = jnp.sum(probs_low.astype(jnp.float32) * dprob, axis=0, keepdims=True)
                dscore = (scale * probs) * (dprob - delta)
                probs_ref[n, :, cols] = probs_low
                dscores_ref[n, :, cols] = dscore.astype(bf16)
                falls_ref[n, i] = jnp.broadcast_to(jnp.sum(dscore, axis=1, keepdims=True), (BUCKET, BUCKET))
        for n, (b, h) in enumerate(todo):
            if h == 0:
                falls = sum(
                    jnp.where(lane == i, falls_ref[b * (HEADS // 2) + i // 2, i % 2], 0.0) for i in range(HEADS)
                ).T
            q, k, g = (part_of(which, b, h) for which in (0, 1, 3))
            dscore_tall = jnp.concatenate([dscores_ref[n, :, :BUCKET], dscores_ref[n, :, BUCKET:]], axis=0)
            dq = dot(blocked(k), dscore_tall, 1, 0)
            fall = jnp.concatenate(
                [jnp.broadcast_to(falls[i : i + 1], (head_dim, BUCKET)) for i in (2 * h, 2 * h + 1)], axis=0
            )
            dk = dot(blocked(q), dscores_ref[n], 1, 1) - fall * k.astype(jnp.float32)
            dv = dot(blocked(g), probs_ref[n], 1, 1)
            for which, grad in enumerate((dq, dk, dv)):
                at = which * feat + h * pair
                grads_ref[at : at + pair, b * BUCKET : (b + 1) * BUCKET] = grad.astype(bf16)
        back = dot(picks, grads_ref[...], 1, 1).astype(bf16).reshape(2, group, span, 3 * feat)
        for part, ref in enumerate((out_own_ref, out_other_ref)):
            ref[:, low:high, :] = ref[:, low:high, :] + back[part]


def call(kernel, out_shape, scratch=(), flops=0, moved=0, in_specs=None, out_specs=None, vmem_bytes=VMEM_BYTES):
    extra = {name: specs for name, specs in (("in_specs", in_specs), ("out_specs", out_specs)) if specs is not None}
    return pl.pallas_call(
        kernel,
        out_shape=out_shape,
        scratch_shapes=list(scratch),
        compiler_params=pltpu.CompilerParams(vmem_limit_bytes=vmem_bytes),
        cost_estimate=pl.CostEstimate(flops=flops, bytes_accessed=moved, transcendentals=0),
        **extra,
    )


def on_device(query, key_rows, value, out_grad, members):
    feat, points = query.shape
    tables = members.shape[0]
    phi, eta = lax.axis_size("phi"), lax.axis_size("eta")
    half = eta // 2
    group = phi * half
    capacity = 5 * points // (4 * phi * eta)
    rows = -(-tables * capacity // 16) * 16
    windows = [(t * capacity // 16 * 16, -(-(t * capacity + capacity) // 16) * 16) for t in range(tables)]
    halves = [[p * eta + h * half + e for p in range(phi) for e in range(half)] for h in range(2)]
    layer = eta // 4
    across = [
        (p * eta + z * layer + e, p * eta + (3 - z) * layer + e) for p in range(phi) for z in range(4) for e in range(layer)
    ]
    bf16 = jnp.bfloat16
    packed = jax.ShapeDtypeStruct((group, rows, 4 * feat), bf16)
    reply = jax.ShapeDtypeStruct((group, rows, 3 * feat), bf16)
    steps = points // BUCKET * (HEADS // 2)
    vmem, hbm = pl.BlockSpec(memory_space=pltpu.VMEM), pl.BlockSpec(memory_space=pl.ANY)

    def exchange(chunks):
        return lax.all_to_all(chunks, AXES, 0, 0, tiled=True, axis_index_groups=halves)

    def pack(part, flops):
        return call(
            functools.partial(pack_kernel, part),
            packed,
            scratch=(
                pltpu.VMEM((4 * feat, points), bf16),
                pltpu.VMEM((PACK_STEPS, group // PACK_STEPS, rows, 4 * feat), bf16),
                pltpu.SemaphoreType.DMA((4,)),
                pltpu.SemaphoreType.DMA((PACK_STEPS,)),
            ),
            out_specs=pl.BlockSpec(memory_space=pl.ANY),
            in_specs=[vmem] + [pl.BlockSpec(memory_space=pltpu.HBM)] * 4,
            flops=flops,
            moved=2 * group * rows * 4 * feat,
            vmem_bytes=WHOLE_VMEM_BYTES,
        )

    arrays = (query, key_rows, value, out_grad)
    copies = [lax.ppermute(array, AXES, across) for array in arrays]

    index = call(
        functools.partial(index_kernel, (windows, capacity, rows, eta)),
        (
            jax.ShapeDtypeStruct((group, 8, 2 * rows), jnp.int32),
            jax.ShapeDtypeStruct((tables, points), jnp.int32),
        ),
        in_specs=[pl.BlockSpec(memory_space=pltpu.SMEM), vmem],
        flops=10**9,
        moved=10**5,
    )
    wanted, codes = index((lax.axis_index("eta") // half).astype(jnp.int32).reshape(1, 1), members)
    wanted = exchange(wanted)

    arrived_own = exchange(pack(0, 2 * group * rows * points * 4 * feat)(wanted, *arrays))
    arrived_other = exchange(pack(1, PACK_FLOPS)(wanted, *copies))
    attend = call(
        functools.partial(attend_kernel, windows),
        (reply, reply),
        scratch=(
            pltpu.VMEM((4 * feat, points), bf16),
            pltpu.VMEM((3 * feat, points), bf16),
            pltpu.VMEM((steps, BUCKET, 2 * BUCKET), jnp.float32),
            pltpu.VMEM((steps, BUCKET, 2 * BUCKET), jnp.float32),
            pltpu.VMEM((steps, BUCKET, 2 * BUCKET), bf16),
            pltpu.VMEM((steps, BUCKET, 2 * BUCKET), bf16),
            pltpu.VMEM((steps, 2, BUCKET, BUCKET), jnp.float32),
        ),
        flops=2 * 10**10,
        moved=8 * 10**6,
    )
    reply_own, reply_other = attend(codes, arrived_own, arrived_other)
    returned_other = exchange(reply_other)
    fold = call(
        fold_kernel,
        jax.ShapeDtypeStruct((3 * feat, points), bf16),
        flops=2 * group * rows * points * 3 * feat,
        moved=2 * group * rows * 3 * feat,
    )
    folded, reply_own = lax.optimization_barrier((fold(wanted, returned_other), reply_own))
    summed = lax.ppermute(folded, AXES, across)
    summed = pl.pallas_call(
        keep_kernel,
        out_shape=jax.ShapeDtypeStruct((3 * feat, points), bf16),
        in_specs=[hbm],
        out_specs=hbm,
        input_output_aliases={0: 0},
        cost_estimate=pl.CostEstimate(flops=PACK_FLOPS, bytes_accessed=0, transcendentals=0),
    )(summed)
    returned_own = exchange(reply_own)
    finish = call(
        finish_kernel,
        (jax.ShapeDtypeStruct((feat, points), jnp.float32),) * 3,
        flops=2 * group * rows * points * 3 * feat,
        moved=2 * group * rows * 3 * feat,
    )
    own_sums = finish(wanted, returned_own)
    return tuple(
        (own + summed[n * feat : (n + 1) * feat].astype(jnp.float32)).astype(bf16) for n, own in enumerate(own_sums)
    )


def solution(mesh):
    split = P(None, AXES)
    in_specs = (split, split, split, split, P(None, AXES, None))
    return jax.shard_map(
        on_device, mesh=mesh, in_specs=in_specs, out_specs=(split, split, split), check_vma=False
    )
```

```python
import functools

import jax
import jax.numpy as jnp
from jax import lax
from jax.experimental import pallas as pl
from jax.experimental.pallas import tpu as pltpu
from jax.sharding import PartitionSpec as P

HEADS = 8
BUCKET = 128
AXES = ("phi", "eta")
LOG2E = 1.4426950408889634
VMEM_BYTES = 48 * 1024 * 1024
WHOLE_VMEM_BYTES = 62 * 1024 * 1024
PACK_FLOPS = 4 * 10**10
PACK_STEPS = 4


def dot(a, b, da, db):
    return lax.dot_general(a, b, (((da,), (db,)), ((), ())), preferred_element_type=jnp.float32)


def column_of(row, first, count):
    n = row.shape[1]
    diagonal = lax.broadcasted_iota(jnp.int32, (count, n), 0) + first == lax.broadcasted_iota(jnp.int32, (count, n), 1)
    return jnp.sum(jnp.where(diagonal, jnp.broadcast_to(row, (count, n)), 0.0), axis=1, keepdims=True)


def slots_of(wanted_ref, part, rows, points, owners=None):
    places = lax.broadcasted_iota(jnp.int32, (rows, points), 1).astype(jnp.float32)
    picks = []
    for o in range(wanted_ref.shape[0]) if owners is None else owners:
        wanted = wanted_ref[o, :1].astype(jnp.float32)
        picks.append(jnp.where(column_of(wanted, part * rows, rows) == places, 1.0, 0.0).astype(jnp.bfloat16))
    return jnp.concatenate(picks, axis=0)


def index_kernel(sizes, half_ref, members_ref, wanted_ref, codes_ref):
    windows, capacity, rows, eta = sizes
    tables, buckets, _ = members_ref.shape
    points = buckets * BUCKET
    group = wanted_ref.shape[0]
    half = eta // 2
    f32, bf16 = jnp.float32, jnp.bfloat16
    ids = jnp.concatenate([members_ref[:, b, :] for b in range(buckets)], axis=1).astype(f32)
    home = jnp.floor((ids + 0.5) * (1.0 / points))
    local = ids - home * points
    home_p = jnp.floor((home + 0.5) * (1.0 / eta))
    home_e = home - home_p * eta
    home_h = jnp.floor((home_e + 0.5) * (1.0 / half))
    part = jnp.where(home_h == half_ref[0, 0].astype(f32), 0.0, 1.0)
    within = home_e - home_h * half
    deep = jnp.floor((within + 0.5) * (2.0 / half))
    place = home_p * half + within + part * (0.5 * half) * (1.0 - 2.0 * deep)
    before = lax.broadcasted_iota(jnp.int32, (points, points), 0) < lax.broadcasted_iota(jnp.int32, (points, points), 1)
    before = jnp.where(before, 1.0, 0.0).astype(bf16)
    homes = lax.broadcasted_iota(jnp.int32, (2 * group, points), 0).astype(f32)
    holders = lax.broadcasted_iota(jnp.int32, (group, points), 0).astype(f32)
    lanes = lax.broadcasted_iota(jnp.int32, (2 * rows, points), 0).astype(f32)
    total = jnp.zeros((2 * group, 2 * rows), f32)
    for t in range(tables):
        row = slice(t, t + 1)
        hot = jnp.where(homes == home[row], 1.0, 0.0)
        rank = jnp.sum(hot * dot(hot.astype(bf16), before, 1, 0), axis=0, keepdims=True)
        slot = rank + float(t * capacity)
        low, high = windows[t]
        code = (part[row] * float(group) + place[row]) * float(high - low) + slot - float(low)
        codes_ref[row, :] = code.astype(jnp.int32)
        named = local[row] + 1.0
        large = jnp.floor(named * (1.0 / 256.0)) * 256.0
        held = holders == place[row]
        values = jnp.concatenate([jnp.where(held, large, 0.0), jnp.where(held, named - large, 0.0)], axis=0)
        at = jnp.where(lanes == part[row] * float(rows) + slot, 1.0, 0.0)
        total += dot(values.astype(bf16), at.astype(bf16), 1, 1)
    wanted = (total[:group] + total[group:] - 1.0).astype(jnp.int32)
    for o in range(group):
        wanted_ref[o] = jnp.broadcast_to(wanted[o : o + 1], wanted_ref.shape[1:])


def pack_kernel(part, wanted_ref, q_ref, k_ref, v_ref, g_ref, out_ref, features_ref, packed_ref, sems, out_sems):
    group, rows, width = out_ref.shape
    feat, points = q_ref.shape
    copies = [
        pltpu.make_async_copy(ref, features_ref.at[pl.ds(n * feat, feat)], sems.at[n])
        for n, ref in enumerate((q_ref, k_ref, v_ref, g_ref))
    ]
    for copy in copies:
        copy.start()
    share = group // PACK_STEPS
    picks = [
        slots_of(wanted_ref, part, rows, points, range(c * share, (c + 1) * share)) for c in range(PACK_STEPS)
    ]
    for copy in copies:
        copy.wait()
    features = features_ref[...]
    results = []
    for c in range(PACK_STEPS):
        packed = dot(picks[c], features, 1, 1).astype(jnp.bfloat16)
        packed_ref[c] = packed.reshape(share, rows, width)
        results.append(
            pltpu.make_async_copy(packed_ref.at[c], out_ref.at[pl.ds(c * share, share)], out_sems.at[c])
        )
        results[-1].start()
    for result in results:
        result.wait()


def fold_kernel(wanted_ref, replies_ref, out_ref):
    group, rows, width = replies_ref.shape
    picks = slots_of(wanted_ref, 1, rows, out_ref.shape[1])
    out_ref[...] = dot(replies_ref[...].reshape(group * rows, width), picks, 0, 0).astype(jnp.bfloat16)


def keep_kernel(in_ref, out_ref):
    pass


def finish_kernel(wanted_ref, replies_ref, q_ref, k_ref, v_ref):
    group, rows, width = replies_ref.shape
    feat, points = q_ref.shape
    picks = slots_of(wanted_ref, 0, rows, points)
    total = dot(replies_ref[...].reshape(group * rows, width), picks, 0, 0)
    for n, ref in enumerate((q_ref, k_ref, v_ref)):
        ref[...] = total[n * feat : (n + 1) * feat]


def attend_kernel(
    windows,
    codes_ref,
    own_ref,
    other_ref,
    result_ref,
    out_other_ref,
    out_own_ref,
    sem,
    feats_ref,
    grads_ref,
    scores_ref,
    dprobs_ref,
    probs_ref,
    dscores_ref,
    falls_ref,
):
    group, rows, width4 = own_ref.shape
    feat = width4 // 4
    head_dim = feat // HEADS
    scale = head_dim**-0.5
    tables, points = codes_ref.shape
    buckets = points // BUCKET
    pair = 2 * head_dim
    bf16 = jnp.bfloat16
    head_of = lax.broadcasted_iota(jnp.int32, (pair, 2 * BUCKET), 0) // head_dim
    block_of = lax.broadcasted_iota(jnp.int32, (pair, 2 * BUCKET), 1) // BUCKET
    mask = jnp.where(head_of == block_of, 1.0, 0.0).astype(bf16)
    tail = lax.broadcasted_iota(jnp.int32, (16, BUCKET), 0)
    tail_wide = lax.broadcasted_iota(jnp.int32, (16, 2 * BUCKET), 0)
    tail_block = lax.broadcasted_iota(jnp.int32, (16, 2 * BUCKET), 1) // BUCKET
    halves = jnp.where((tail_wide < 6) & (tail_wide // 3 == tail_block), -0.5, 0.0).astype(bf16)
    lane = lax.broadcasted_iota(jnp.int32, (BUCKET, BUCKET), 1)

    def blocked(part):
        return jnp.concatenate([part, part], axis=1) * mask

    def norm_rows(k):
        wide = k.astype(jnp.float32)
        squares = wide * wide
        first, second = (
            jnp.sum(squares[i * head_dim : (i + 1) * head_dim], axis=0, keepdims=True) for i in range(2)
        )
        norm = jnp.where(tail < 3, first, second)
        high = norm.astype(bf16).astype(jnp.float32)
        rest = norm - high
        middle = rest.astype(bf16).astype(jnp.float32)
        piece = tail % 3
        out = jnp.where(piece == 0, high, jnp.where(piece == 1, middle, rest - middle))
        return jnp.where(tail < 6, out, 0.0).astype(bf16)

    out_own_ref[...] = jnp.zeros_like(out_own_ref)
    out_other_ref[...] = jnp.zeros_like(out_other_ref)
    todo = [(b, h) for b in range(buckets) for h in range(HEADS // 2)]
    for t in range(tables):
        low, high = windows[t]
        span = high - low
        slots = 2 * group * span
        codes = codes_ref[t : t + 1, :].astype(jnp.float32)
        places = lax.broadcasted_iota(jnp.int32, (slots, points), 0).astype(jnp.float32)
        picks = jnp.where(places == codes, 1.0, 0.0).astype(bf16)
        arrived = jnp.concatenate(
            [ref[:, low:high, :].reshape(group * span, width4) for ref in (own_ref, other_ref)], axis=0
        )
        feats_ref[...] = dot(arrived, picks, 0, 0).astype(bf16)

        def part_of(which, b, h):
            at = which * feat + h * pair
            return feats_ref[at : at + pair, b * BUCKET : (b + 1) * BUCKET]

        for n, (b, h) in enumerate(todo):
            q, k, v, g = (part_of(which, b, h) for which in range(4))
            scores_ref[n] = dot(
                jnp.concatenate([k, norm_rows(k)], axis=0), jnp.concatenate([blocked(q), halves], axis=0), 0, 0
            )
            dprobs_ref[n] = dot(v, blocked(g), 0, 0)
        for n in range(len(todo)):
            for i in range(2):
                cols = slice(i * BUCKET, (i + 1) * BUCKET)
                dprob = dprobs_ref[n, :, cols]
                scores = scores_ref[n, :, cols]
                expons = jnp.exp2((scores - jnp.max(scores, axis=0, keepdims=True)) * (scale * LOG2E))
                probs = expons * (1.0 / jnp.sum(expons, axis=0, keepdims=True))
                probs_low = probs.astype(bf16)
                delta = jnp.sum(probs_low.astype(jnp.float32) * dprob, axis=0, keepdims=True)
                dscore = (scale * probs) * (dprob - delta)
                probs_ref[n, :, cols] = probs_low
                dscores_ref[n, :, cols] = dscore.astype(bf16)
                falls_ref[n, i] = jnp.broadcast_to(jnp.sum(dscore, axis=1, keepdims=True), (BUCKET, BUCKET))
        for n, (b, h) in enumerate(todo):
            if h == 0:
                falls = sum(
                    jnp.where(lane == i, falls_ref[b * (HEADS // 2) + i // 2, i % 2], 0.0) for i in range(HEADS)
                ).T
            q, k, g = (part_of(which, b, h) for which in (0, 1, 3))
            dscore_tall = jnp.concatenate([dscores_ref[n, :, :BUCKET], dscores_ref[n, :, BUCKET:]], axis=0)
            dq = dot(blocked(k), dscore_tall, 1, 0)
            fall = jnp.concatenate(
                [jnp.broadcast_to(falls[i : i + 1], (head_dim, BUCKET)) for i in (2 * h, 2 * h + 1)], axis=0
            )
            dk = dot(blocked(q), dscores_ref[n], 1, 1) - fall * k.astype(jnp.float32)
            dv = dot(blocked(g), probs_ref[n], 1, 1)
            for which, grad in enumerate((dq, dk, dv)):
                at = which * feat + h * pair
                grads_ref[at : at + pair, b * BUCKET : (b + 1) * BUCKET] = grad.astype(bf16)
        grads = grads_ref[...]
        for part, ref in enumerate((out_own_ref, out_other_ref)):
            back = dot(picks[part * group * span : (part + 1) * group * span], grads, 1, 1).astype(bf16)
            ref[:, low:high, :] = ref[:, low:high, :] + back.reshape(group, span, 3 * feat)
            if t == tables - 1 and part == 0:
                copy = pltpu.make_async_copy(out_own_ref, result_ref, sem)
                copy.start()
    copy.wait()


def call(kernel, out_shape, scratch=(), flops=0, moved=0, in_specs=None, out_specs=None, vmem_bytes=VMEM_BYTES):
    extra = {name: specs for name, specs in (("in_specs", in_specs), ("out_specs", out_specs)) if specs is not None}
    return pl.pallas_call(
        kernel,
        out_shape=out_shape,
        scratch_shapes=list(scratch),
        compiler_params=pltpu.CompilerParams(vmem_limit_bytes=vmem_bytes),
        cost_estimate=pl.CostEstimate(flops=flops, bytes_accessed=moved, transcendentals=0),
        **extra,
    )


def on_device(query, key_rows, value, out_grad, members):
    feat, points = query.shape
    tables = members.shape[0]
    phi, eta = lax.axis_size("phi"), lax.axis_size("eta")
    half = eta // 2
    group = phi * half
    capacity = 5 * points // (4 * phi * eta)
    rows = -(-tables * capacity // 16) * 16
    windows = [(t * capacity // 16 * 16, -(-(t * capacity + capacity) // 16) * 16) for t in range(tables)]
    halves = [[p * eta + h * half + e for p in range(phi) for e in range(half)] for h in range(2)]
    layer = eta // 4
    across = [
        (p * eta + z * layer + e, p * eta + (3 - z) * layer + e) for p in range(phi) for z in range(4) for e in range(layer)
    ]
    bf16 = jnp.bfloat16
    packed = jax.ShapeDtypeStruct((group, rows, 4 * feat), bf16)
    reply = jax.ShapeDtypeStruct((group, rows, 3 * feat), bf16)
    steps = points // BUCKET * (HEADS // 2)
    vmem, hbm = pl.BlockSpec(memory_space=pltpu.VMEM), pl.BlockSpec(memory_space=pl.ANY)

    def exchange(chunks):
        return lax.all_to_all(chunks, AXES, 0, 0, tiled=True, axis_index_groups=halves)

    def pack(part, flops):
        return call(
            functools.partial(pack_kernel, part),
            packed,
            scratch=(
                pltpu.VMEM((4 * feat, points), bf16),
                pltpu.VMEM((PACK_STEPS, group // PACK_STEPS, rows, 4 * feat), bf16),
                pltpu.SemaphoreType.DMA((4,)),
                pltpu.SemaphoreType.DMA((PACK_STEPS,)),
            ),
            out_specs=pl.BlockSpec(memory_space=pl.ANY),
            in_specs=[vmem] + [pl.BlockSpec(memory_space=pltpu.HBM)] * 4,
            flops=flops,
            moved=2 * group * rows * 4 * feat,
            vmem_bytes=WHOLE_VMEM_BYTES,
        )

    arrays = (query, key_rows, value, out_grad)
    copies = [lax.ppermute(array, AXES, across) for array in arrays]

    index = call(
        functools.partial(index_kernel, (windows, capacity, rows, eta)),
        (
            jax.ShapeDtypeStruct((group, 8, 2 * rows), jnp.int32),
            jax.ShapeDtypeStruct((tables, points), jnp.int32),
        ),
        in_specs=[pl.BlockSpec(memory_space=pltpu.SMEM), vmem],
        flops=10**9,
        moved=10**5,
    )
    wanted, codes = index((lax.axis_index("eta") // half).astype(jnp.int32).reshape(1, 1), members)
    wanted = exchange(wanted)

    arrived_own = exchange(pack(0, 2 * group * rows * points * 4 * feat)(wanted, *arrays))
    arrived_other = exchange(pack(1, PACK_FLOPS)(wanted, *copies))
    attend = call(
        functools.partial(attend_kernel, windows),
        (reply, reply),
        in_specs=[vmem] * 3,
        out_specs=(hbm, vmem),
        scratch=(
            pltpu.VMEM(reply.shape, bf16),
            pltpu.SemaphoreType.DMA,
            pltpu.VMEM((4 * feat, points), bf16),
            pltpu.VMEM((3 * feat, points), bf16),
            pltpu.VMEM((steps, BUCKET, 2 * BUCKET), jnp.float32),
            pltpu.VMEM((steps, BUCKET, 2 * BUCKET), jnp.float32),
            pltpu.VMEM((steps, BUCKET, 2 * BUCKET), bf16),
            pltpu.VMEM((steps, BUCKET, 2 * BUCKET), bf16),
            pltpu.VMEM((steps, 2, BUCKET, BUCKET), jnp.float32),
        ),
        flops=2 * 10**10,
        moved=8 * 10**6,
    )
    reply_own, reply_other = attend(codes, arrived_own, arrived_other)
    returned_other = exchange(reply_other)
    fold = call(
        fold_kernel,
        jax.ShapeDtypeStruct((3 * feat, points), bf16),
        flops=2 * group * rows * points * 3 * feat,
        moved=2 * group * rows * 3 * feat,
    )
    folded, reply_own = lax.optimization_barrier((fold(wanted, returned_other), reply_own))
    summed = lax.ppermute(folded, AXES, across)
    summed = pl.pallas_call(
        keep_kernel,
        out_shape=jax.ShapeDtypeStruct((3 * feat, points), bf16),
        in_specs=[hbm],
        out_specs=hbm,
        input_output_aliases={0: 0},
        cost_estimate=pl.CostEstimate(flops=PACK_FLOPS, bytes_accessed=0, transcendentals=0),
    )(summed)
    returned_own = exchange(reply_own)
    finish = call(
        finish_kernel,
        (jax.ShapeDtypeStruct((feat, points), jnp.float32),) * 3,
        flops=2 * group * rows * points * 3 * feat,
        moved=2 * group * rows * 3 * feat,
    )
    own_sums = finish(wanted, returned_own)
    return tuple(
        (own + summed[n * feat : (n + 1) * feat].astype(jnp.float32)).astype(bf16) for n, own in enumerate(own_sums)
    )


def solution(mesh):
    split = P(None, AXES)
    in_specs = (split, split, split, split, P(None, AXES, None))
    return jax.shard_map(
        on_device, mesh=mesh, in_specs=in_specs, out_specs=(split, split, split), check_vma=False
    )
```
